512 devices in a mesh: hid: 64 (over z, x), mdl: 8 (over y, core).
Axes of the slice: x: 4, y: 4, z: 16, core: 2. Of those that a mesh axis runs over, the one named last changes fastest.
Arguments:
- inputs: bfloat16 [768, 8192], P('hid', 'mdl'), may hold values from -6 to 6
- cotangent: bfloat16 [768, 8192], P('hid', 'mdl'), may hold values from -6 to 6
- w_gate: bfloat16 [8192, 16384], P('mdl', 'hid'), may hold values from -0.0625 to 0.0625
- w_up: bfloat16 [8192, 16384], P('mdl', 'hid'), may hold values from -0.0625 to 0.0625
- w_down: bfloat16 [16384, 8192], P('hid', 'mdl'), may hold values from -0.046875 to 0.046875
- keep_mask: int32 [12, 128], P(None, 'hid'), may hold values 0 or 1
Outputs:
- grad_input: bfloat16 [768, 8192], P('hid', 'mdl')
- grad_gate: bfloat16 [8192, 16384], P('mdl', 'hid')
- grad_up: bfloat16 [8192, 16384], P('mdl', 'hid')
- grad_down: bfloat16 [16384, 8192], P('hid', 'mdl')
The draws below stay inside these ranges and needn't reach their ends.
All inputs are finite; a program needn't handle non-finite values. No bound on the sum of `keep_mask` on one device may be relied on, other than what follows from the above.
Results may differ from the reference program's by a relative error of at most 0.0049.
Values may be sent and summed in bfloat16 or wider, within the bound.
No kernel may reach another device: no remote copies, remote signals or barrier semaphores. Data moves between devices by JAX's collectives and lax.ppermute only.
A program may use at most 64 MiB of HBM per device.

```python
import jax
import jax.numpy as jnp
from jax import lax

D = 8192
FF = 16384
BLOCK = 128
TILE = 64
TOKENS = 768
TILES = 12
BLOCKS = 128


def set_ends(drawn, own_key, low, largest):
    extent = drawn.shape
    spot = [jax.random.randint(jax.random.fold_in(own_key, axis), (), 0, extent[axis]) for axis in range(len(extent))]
    drawn = drawn.at[tuple(spot)].set(low)
    longest = extent.index(max(extent))
    spot[longest] = (spot[longest] + 1) % extent[longest]
    return drawn.at[tuple(spot)].set(largest)


def shard_levels(key, extent, shards, least, largest):
    gain = 1.0
    for position, shards_of in shards:
        steps = jax.random.uniform(jax.random.fold_in(jax.random.fold_in(key, 6), position), (shards_of,), jnp.float32, least / len(shards), largest / len(shards))
        gain = gain * jnp.repeat(jnp.exp(steps), extent[position] // shards_of).reshape((-1,) + (1,) * (len(extent) - 1 - position))
    return gain


def gaussian(rng, extent, deviation, reach, shards=(), dtype=jnp.bfloat16):
    level = shard_levels(rng, extent, shards, -0.22, 0.18) if shards else 1.0
    entries = jax.random.normal(rng, extent, jnp.float32) * deviation * level
    return jnp.minimum(jnp.maximum(entries, -reach), reach).astype(dtype)


def setup_inputs(seed: int = 0) -> dict:
    key_list = jax.random.split(jax.random.key(seed), 7)
    inputs = gaussian(key_list[0], (TOKENS, D), 1.0, 6.0, ((0, 64), (1, 8)))
    cotangent = gaussian(key_list[1], (TOKENS, D), 1.0, 6.0, ((0, 64), (1, 8)))
    w_gate = gaussian(key_list[2], (D, FF), D ** -0.5, 0.0625, ((0, 8), (1, 64)))
    w_up = gaussian(key_list[3], (D, FF), D ** -0.5, 0.0625, ((0, 8), (1, 64)))
    w_down = gaussian(key_list[4], (FF, D), FF ** -0.5, 0.046875, ((0, 64), (1, 8)))
    keep_mask = set_ends((jax.random.randint(key_list[5], (TILES, BLOCKS), 0, 5) < 2).astype(jnp.int32), jax.random.fold_in(key_list[5], 1), 0, 1)
    return {"inputs": inputs, "cotangent": cotangent, "w_gate": w_gate, "w_up": w_up, "w_down": w_down, "keep_mask": keep_mask}


def pointwise_parts(gate_pre, up_pre, grad_hidden, keep_full):
    sigmoid_gate = jax.nn.sigmoid(gate_pre)
    silu_gate = gate_pre * sigmoid_gate
    hidden_kept = (silu_gate * up_pre * keep_full).astype(jnp.bfloat16)
    slope = sigmoid_gate * (1.0 + gate_pre * (1.0 - sigmoid_gate))
    grad_gate_pre = (grad_hidden * up_pre * slope).astype(jnp.bfloat16)
    grad_up_pre = (grad_hidden * silu_gate).astype(jnp.bfloat16)
    return hidden_kept, grad_gate_pre, grad_up_pre


def reference(inputs, cotangent, w_gate, w_up, w_down, keep_mask):
    inner = (((1,), (1,)), ((), ()))
    outer = (((0,), (0,)), ((), ()))
    gate_pre = jnp.dot(inputs, w_gate, preferred_element_type=jnp.float32)
    up_pre = jnp.dot(inputs, w_up, preferred_element_type=jnp.float32)
    grad_hidden = lax.dot_general(cotangent, w_down, inner, preferred_element_type=jnp.float32)
    keep_full = jnp.repeat(jnp.repeat(keep_mask, TILE, axis=0), BLOCK, axis=1).astype(jnp.float32)
    hidden_kept, grad_gate_pre, grad_up_pre = pointwise_parts(gate_pre, up_pre, grad_hidden, keep_full)
    grad_down = lax.dot_general(hidden_kept, cotangent, outer, preferred_element_type=jnp.float32).astype(jnp.bfloat16)
    grad_gate = lax.dot_general(inputs, grad_gate_pre, outer, preferred_element_type=jnp.float32).astype(jnp.bfloat16)
    grad_up = lax.dot_general(inputs, grad_up_pre, outer, preferred_element_type=jnp.float32).astype(jnp.bfloat16)
    grad_input = lax.dot_general(grad_gate_pre, w_gate, inner, preferred_element_type=jnp.float32)
    grad_input = grad_input + lax.dot_general(grad_up_pre, w_up, inner, preferred_element_type=jnp.float32)
    return grad_input.astype(jnp.bfloat16), grad_gate, grad_up, grad_down
```

```python
import jax
import jax.numpy as jnp
from jax import lax
from jax.sharding import Mesh, PartitionSpec as P

F32, BF16 = jnp.float32, jnp.bfloat16
INNER = (((1,), (1,)), ((), ()))
OUTER = (((0,), (0,)), ((), ()))
ALONG_X = (0, -1, 1, 2)


def ring(size, step):
    return [(i, (i + step) % size) for i in range(size)]


def dot(a, b, dims):
    return lax.dot_general(a, b, dims, preferred_element_type=F32)


def pointwise_parts(gate_pre, up_pre, grad_hidden, keep_rows):
    sigmoid_gate = jax.nn.sigmoid(gate_pre)
    silu_gate = gate_pre * sigmoid_gate
    hidden_kept = (silu_gate * up_pre * keep_rows).astype(BF16)
    slope = sigmoid_gate * (1.0 + gate_pre * (1.0 - sigmoid_gate))
    grad_gate_pre = (grad_hidden * up_pre * slope).astype(BF16)
    grad_up_pre = (grad_hidden * silu_gate).astype(BF16)
    return hidden_kept, grad_gate_pre, grad_up_pre


def keep_of_rows(keep_mask, rows, own_tokens, nz, nx, total):
    tiles, blocks = keep_mask.shape
    part = lax.axis_index("c") * 4 + lax.axis_index("y")
    place = part * rows + lax.broadcasted_iota(jnp.int32, (rows, 1), 0)
    per_chunk = nz * own_tokens
    chunk, inside = place // per_chunk, place % per_chunk
    shift = jnp.where(chunk == 1, -1, jnp.where(chunk == 2, 1, jnp.where(chunk == 3, 2, 0)))
    from_x = (lax.axis_index("x") + shift + nx) % nx
    token = (inside // own_tokens * nx + from_x) * own_tokens + inside % own_tokens
    tile = token // (total // tiles)
    chosen = tile == lax.broadcasted_iota(jnp.int32, (rows, tiles), 1)
    keep = [
        jnp.sum(jnp.where(chosen, keep_mask[:, b][None, :], 0), axis=1, keepdims=True)
        for b in range(blocks)
    ]
    return jnp.concatenate([jnp.broadcast_to(k, (rows, 128)) for k in keep], axis=1).astype(F32)


def shards(inputs, cotangent, w_gate, w_up, w_down, keep_mask):
    own_tokens, width = inputs.shape
    hidden = w_gate.shape[1]
    nz, nx, ny, nc = 16, 4, 4, 2
    total = own_tokens * nz * nx
    rows = total // (ny * nc)
    flat = own_tokens * width // 128

    keep_rows = keep_of_rows(keep_mask, rows, own_tokens, nz, nx, total)

    packed = jnp.concatenate([inputs.reshape(flat, 128), cotangent.reshape(flat, 128)])
    along_z = lax.all_gather(packed, ("zh", "zl"))
    own = [along_z[:, i * flat : (i + 1) * flat].reshape(nz * own_tokens, width) for i in range(2)]
    own = jnp.stack(own)
    right = lax.ppermute(own, "x", ring(nx, 1))
    left = lax.ppermute(own, "x", ring(nx, -1))
    far_in = lax.ppermute(right[0], "x", ring(nx, 1))
    far_cot = lax.ppermute(left[1], "x", ring(nx, -1))
    x_parts = [own[0], right[0], left[0], far_in]
    c_parts = [own[1], right[1], left[1], far_cot]
    all_inputs = jnp.concatenate(x_parts)
    all_cotangent = jnp.concatenate(c_parts)

    part_gate = dot(all_inputs, w_gate, (((1,), (0,)), ((), ())))
    part_up = dot(all_inputs, w_up, (((1,), (0,)), ((), ())))
    part_hidden = dot(all_cotangent, w_down, INNER)
    parts = jnp.stack(
        [p.reshape(nc, ny, rows, hidden) for p in (part_gate, part_up, part_hidden)], axis=2
    )
    summed = jnp.sum(lax.all_to_all(parts, "c", 0, 0), axis=0)
    summed = jnp.sum(lax.all_to_all(summed, "y", 0, 0), axis=0)
    hidden_kept, grad_gate_pre, grad_up_pre = pointwise_parts(
        summed[0], summed[1], summed[2], keep_rows
    )

    def over_mdl(a):
        return lax.all_gather(lax.all_gather(a, "y"), "c")

    both = over_mdl(jnp.stack([grad_gate_pre, grad_up_pre]))
    all_gate = both[:, :, 0].reshape(total, hidden)
    all_up = both[:, :, 1].reshape(total, hidden)
    all_kept = over_mdl(hidden_kept).reshape(total, hidden)

    result = (dot(all_gate, w_gate, INNER) + dot(all_up, w_up, INNER)).astype(BF16)
    result = result.reshape(nx, nz * own_tokens, width)
    arrived = [lax.ppermute(result[k], "x", ring(nx, ALONG_X[k])) for k in (1, 2, 3)]
    kept = result[0].astype(F32) + sum(a.astype(F32) for a in arrived)
    kept = kept.astype(BF16).reshape(4, 4, flat, 128).transpose(1, 0, 2, 3)
    kept = jnp.sum(lax.all_to_all(kept, "zl", 0, 0).astype(F32), axis=0).astype(BF16)
    kept = jnp.sum(lax.all_to_all(kept, "zh", 0, 0).astype(F32), axis=0).astype(BF16)
    grad_input = kept.reshape(own_tokens, width)

    grad_down = dot(all_kept, all_cotangent, OUTER).astype(BF16)
    grad_gate = dot(all_inputs, all_gate, OUTER).astype(BF16)
    grad_up = dot(all_inputs, all_up, OUTER).astype(BF16)
    return grad_input, grad_gate, grad_up, grad_down


def solution(mesh):
    fine = Mesh(mesh.devices.reshape(4, 4, 4, 4, 2), ("zh", "zl", "x", "y", "c"))
    hid, mdl = ("zh", "zl", "x"), ("y", "c")
    placed = (P(hid, mdl), P(hid, mdl), P(mdl, hid), P(mdl, hid), P(hid, mdl), P(None, hid))
    return jax.shard_map(
        shards,
        mesh=fine,
        in_specs=placed,
        out_specs=(P(hid, mdl), P(mdl, hid), P(mdl, hid), P(hid, mdl)),
        check_vma=False,
    )
```

```python
import functools

import jax
import jax.numpy as jnp
from jax import lax
from jax.experimental import pallas as pl
from jax.experimental.pallas import tpu as pltpu
from jax.sharding import Mesh, PartitionSpec as P

F32, BF16 = jnp.float32, jnp.bfloat16
INNER = (((1,), (1,)), ((), ()))
PLAIN = (((1,), (0,)), ((), ()))
OUTER = (((0,), (0,)), ((), ()))


def ring(size, step):
    return [(i, (i + step) % size) for i in range(size)]


def dot(a, b, dims):
    return lax.dot_general(a, b, dims, preferred_element_type=F32)


def pointwise_parts(gate_pre, up_pre, grad_hidden, keep_rows):
    sigmoid_gate = jax.nn.sigmoid(gate_pre)
    silu_gate = gate_pre * sigmoid_gate
    hidden_kept = (silu_gate * up_pre * keep_rows).astype(BF16)
    slope = sigmoid_gate * (1.0 + gate_pre * (1.0 - sigmoid_gate))
    grad_gate_pre = (grad_hidden * up_pre * slope).astype(BF16)
    grad_up_pre = (grad_hidden * silu_gate).astype(BF16)
    return hidden_kept, grad_gate_pre, grad_up_pre


def keep_of_rows(keep_mask, rows, own_tokens, nx, total):
    tiles, blocks = keep_mask.shape
    chunk = lax.axis_index("y")
    inside = lax.axis_index("c") * rows + lax.broadcasted_iota(jnp.int32, (rows, 1), 0)
    shift = jnp.where(chunk == 1, -1, jnp.where(chunk == 2, 1, jnp.where(chunk == 3, 2, 0)))
    from_x = (lax.axis_index("x") + shift + nx) % nx
    token = (inside // own_tokens * nx + from_x) * own_tokens + inside % own_tokens
    tile = token // (total // tiles)
    chosen = tile == lax.broadcasted_iota(jnp.int32, (rows, tiles), 1)
    keep = [
        jnp.sum(jnp.where(chosen, keep_mask[:, b][None, :], 0), axis=1, keepdims=True)
        for b in range(blocks)
    ]
    return jnp.concatenate([jnp.broadcast_to(k, (rows, 128)) for k in keep], axis=1).astype(F32)


def forward_kernel(rows, x_ref, c_ref, wg_ref, wu_ref, wd_ref, *rest):
    out_ref = rest[-1]
    x, c = x_ref[...], c_ref[...]
    for place, value in enumerate(
        (dot(x, wg_ref[...], PLAIN), dot(x, wu_ref[...], PLAIN), dot(c, wd_ref[...], INNER))
    ):
        out_ref[0, place] = value[:rows]
        out_ref[1, place] = value[rows:]


def forward(chunk, x, c, weights, held, chunks):
    tokens, width = x.shape[-2:]
    hidden = weights[0].shape[1]
    rows = tokens // 2

    def half(a, which):
        if a.ndim == 2:
            return pl.BlockSpec((tokens, width), lambda i: (0, 0))
        return pl.BlockSpec((None, tokens, width), lambda i: (which, 0, 0))

    whole = [pl.BlockSpec(w.shape, lambda i: (0, 0)) for w in weights]
    operands, specs, alias = [x, c, *weights], [half(x, 0), half(c, 1), *whole], {}
    if held is not None:
        operands.append(held)
        specs.append(pl.BlockSpec(memory_space=pl.ANY))
        alias = {5: 0}
    return pl.pallas_call(
        functools.partial(forward_kernel, rows),
        out_shape=jax.ShapeDtypeStruct((2, chunks, 3, rows, hidden), F32),
        grid=(1,),
        in_specs=specs,
        out_specs=pl.BlockSpec((2, None, 3, rows, hidden), lambda i: (0, chunk, 0, 0, 0)),
        input_output_aliases=alias,
        compiler_params=pltpu.CompilerParams(vmem_limit_bytes=32 << 20),
        cost_estimate=pl.CostEstimate(
            flops=6 * tokens * width * hidden,
            bytes_accessed=4 * tokens * width + 6 * width * hidden + 12 * tokens * hidden,
            transcendentals=0,
        ),
        name="forward_chunk",
    )(*operands)


def input_grad_kernel(x_index, g_ref, wg_ref, wu_ref, out_ref):
    tokens = out_ref.shape[0]
    hidden = g_ref.shape[-1]
    grad_gate, grad_up = (g_ref[:, i].reshape(tokens, hidden) for i in range(2))
    total = dot(grad_gate, wg_ref[...], INNER) + dot(grad_up, wu_ref[...], INNER)
    out_ref[...] = total.astype(out_ref.dtype)


def input_grad(both, w_gate, w_up, chunks):
    parts, _, rows, hidden = both.shape
    width = w_gate.shape[0]
    tokens = parts * rows // chunks
    place = jnp.array([0, 2, 3, 1], jnp.int32)
    x = lax.axis_index("x")
    order = jnp.stack([place[(d - x + chunks) % chunks] for d in range(chunks)])
    whole = pl.BlockSpec((width, hidden), lambda d, order: (0, 0))
    return pl.pallas_call(
        input_grad_kernel,
        out_shape=jax.ShapeDtypeStruct((chunks, tokens, width), BF16),
        grid_spec=pltpu.PrefetchScalarGridSpec(
            num_scalar_prefetch=1,
            grid=(chunks,),
            in_specs=[
                pl.BlockSpec(
                    (parts // chunks, 2, rows, hidden), lambda d, order: (order[d], 0, 0, 0)
                ),
                whole,
                whole,
            ],
            out_specs=pl.BlockSpec((None, tokens, width), lambda d, order: (d, 0, 0)),
        ),
        compiler_params=pltpu.CompilerParams(vmem_limit_bytes=32 << 20),
        cost_estimate=pl.CostEstimate(
            flops=4 * chunks * tokens * width * hidden,
            bytes_accessed=4 * chunks * tokens * hidden + 4 * width * hidden + 2 * chunks * tokens * width,
            transcendentals=0,
        ),
        name="input_grad",
    )(order, both, w_gate, w_up)


def shards(inputs, cotangent, w_gate, w_up, w_down, keep_mask):
    own_tokens, width = inputs.shape
    hidden = w_gate.shape[1]
    nz, nx, nc = 16, 4, 2
    total = own_tokens * nz * nx
    tokens = own_tokens * nz
    rows = tokens // nc
    flat = own_tokens * width // 128
    weights = (w_gate, w_up, w_down)

    packed = jnp.concatenate([inputs.reshape(flat, 128), cotangent.reshape(flat, 128)])
    along_z = lax.all_gather(packed, "z")
    own = jnp.stack(
        [along_z[:, i * flat : (i + 1) * flat].reshape(tokens, width) for i in range(2)]
    )
    right = lax.ppermute(own, "x", ring(nx, 1))
    left = lax.ppermute(own, "x", ring(nx, -1))
    far_in = lax.ppermute(right[0], "x", ring(nx, 1))
    far_cot = lax.ppermute(left[1], "x", ring(nx, -1))

    parts = forward(0, own, own, weights, None, nx)
    parts = forward(1, right, right, weights, parts, nx)
    parts = forward(2, left, left, weights, parts, nx)
    parts = forward(3, far_in, far_cot, weights, parts, nx)

    summed = jnp.sum(lax.all_to_all(parts, "c", 0, 0), axis=0)
    summed = jnp.sum(lax.all_to_all(summed, "y", 0, 0), axis=0)
    keep_rows = keep_of_rows(keep_mask, rows, own_tokens, nx, total)
    hidden_kept, grad_gate_pre, grad_up_pre = pointwise_parts(
        summed[0], summed[1], summed[2], keep_rows
    )
    both = lax.all_gather(jnp.stack([grad_gate_pre, grad_up_pre]), ("y", "c"))

    result = input_grad(both, w_gate, w_up, nx)
    result, hidden_kept = lax.optimization_barrier((result, hidden_kept))
    arrived = lax.all_to_all(result, "x", 0, 0)
    all_kept = lax.all_gather(hidden_kept, ("y", "c")).reshape(total, hidden)
    all_inputs = jnp.concatenate([own[0], right[0], left[0], far_in])
    all_cotangent = jnp.concatenate([own[1], right[1], left[1], far_cot])
    arrived, all_kept, all_inputs, all_cotangent = lax.optimization_barrier(
        (arrived, all_kept, all_inputs, all_cotangent)
    )
    kept = jnp.sum(arrived.astype(F32), axis=0).astype(BF16).reshape(nz, flat, 128)
    kept, all_kept, all_inputs, all_cotangent, both = lax.optimization_barrier(
        (kept, all_kept, all_inputs, all_cotangent, both)
    )
    kept = jnp.sum(lax.all_to_all(kept, "z", 0, 0).astype(F32), axis=0).astype(BF16)
    grad_input = kept.reshape(own_tokens, width)

    all_gate = both[:, 0].reshape(total, hidden)
    all_up = both[:, 1].reshape(total, hidden)
    grad_down = dot(all_kept, all_cotangent, OUTER).astype(BF16)
    grad_gate = dot(all_inputs, all_gate, OUTER).astype(BF16)
    grad_up = dot(all_inputs, all_up, OUTER).astype(BF16)
    return grad_input, grad_gate, grad_up, grad_down


def solution(mesh):
    fine = Mesh(mesh.devices.reshape(16, 4, 4, 2), ("z", "x", "y", "c"))
    hid, mdl = ("z", "x"), ("y", "c")
    placed = (P(hid, mdl), P(hid, mdl), P(mdl, hid), P(mdl, hid), P(hid, mdl), P(None, hid))
    return jax.shard_map(
        shards,
        mesh=fine,
        in_specs=placed,
        out_specs=(P(hid, mdl), P(mdl, hid), P(mdl, hid), P(hid, mdl)),
        check_vma=False,
    )
```

```python
import functools

import jax
import jax.numpy as jnp
from jax import lax
from jax.experimental import pallas as pl
from jax.experimental.pallas import tpu as pltpu
from jax.sharding import Mesh, PartitionSpec as P

F32, BF16, I16 = jnp.float32, jnp.bfloat16, jnp.int16
INNER = (((1,), (1,)), ((), ()))
PLAIN = (((1,), (0,)), ((), ()))
OUTER = (((0,), (0,)), ((), ()))
SUMS = 3
SCALES = 16
PARAMS = pltpu.CompilerParams(vmem_limit_bytes=32 << 20)


def ring(size, step):
    return [(i, (i + step) % size) for i in range(size)]


def dot(a, b, dims):
    return lax.dot_general(a, b, dims, preferred_element_type=F32)


def cost(flops, moved):
    return pl.CostEstimate(flops=flops, bytes_accessed=moved, transcendentals=0)


def row_is_lane(rows, lanes):
    shape = (rows, lanes)
    return lax.broadcasted_iota(jnp.int32, shape, 0) == lax.broadcasted_iota(jnp.int32, shape, 1)


def code(values):
    rows, lanes = values[0].shape
    diagonal = row_is_lane(rows, lanes)
    place = lax.broadcasted_iota(jnp.int32, (SCALES, lanes), 0)
    codes, tile = [], jnp.zeros((SCALES, lanes), F32)
    for k, v in enumerate(values):
        most = jnp.max(jnp.abs(v), axis=1, keepdims=True)
        exponent = jnp.ceil(jnp.log2(jnp.maximum(most, 1e-30)) + 0.01)
        codes.append(jnp.round(v * jnp.exp2(15.0 - exponent)).astype(jnp.int32).astype(I16))
        along = jnp.sum(jnp.where(diagonal, exponent, 0.0), axis=0, keepdims=True)
        tile = jnp.where(place == k, along, tile)
    return codes, tile.astype(jnp.int32).astype(I16)


def decode(block, rows):
    lanes = block.shape[1]
    diagonal = row_is_lane(rows, lanes)
    tile = jnp.exp2(block[SUMS * rows :].astype(jnp.int32).astype(F32) - 15.0)
    out = []
    for k in range(SUMS):
        scale = jnp.sum(jnp.where(diagonal, tile[k : k + 1], 0.0), axis=1, keepdims=True)
        out.append(block[k * rows : (k + 1) * rows].astype(jnp.int32).astype(F32) * scale)
    return out


def put(out_ref, index, values, rows):
    codes, tile = code(values)
    for k, c in enumerate(codes):
        out_ref[(*index, pl.ds(k * rows, rows))] = c
    out_ref[(*index, pl.ds(SUMS * rows, SCALES))] = tile


def unpack_kernel(packed_ref, out_ref):
    blocks = packed_ref.shape[0]
    width = out_ref.shape[2]
    half = width // 2
    for first in range(0, blocks, 2):
        pair = [packed_ref[first + i].astype(F32) for i in range(2)]
        for which in range(2):
            part = [p[which * 8 : which * 8 + 8] for p in pair]
            out_ref[which, first * 8 : first * 8 + 16] = jnp.concatenate(
                [p[:, :width] for p in part]
            ).astype(BF16)
    for first in range(0, blocks, 4):
        four = [packed_ref[first + i, :, width:].astype(F32) for i in range(4)]
        for which in range(2):
            part = [p[which * 8 : which * 8 + 8] for p in four]
            rows = jnp.concatenate(
                [
                    jnp.concatenate([p[:4] for p in part]),
                    jnp.concatenate([p[4:] for p in part]),
                ],
                axis=1,
            )
            out_ref[which, blocks * 8 + first * 4 : blocks * 8 + first * 4 + 16] = rows.astype(BF16)


def pack(a):
    half = a.shape[1] // 2
    return jnp.concatenate([a[:8], jnp.concatenate([a[8:, :half], a[8:, half:]])], axis=1)


def forward_kernel(rows, x_ref, c_ref, wg_ref, wu_ref, wd_ref, *rest):
    out_ref = rest[-1]
    x, c = x_ref[...], c_ref[...]
    values = [
        dot(x, wg_ref[...], PLAIN),
        dot(x, wu_ref[...], PLAIN),
        dot(c, wd_ref[...], INNER),
    ]
    for core in range(2):
        put(out_ref, (core,), [v[core * rows : (core + 1) * rows] for v in values], rows)


def forward(chunk, x, c, weights, held, chunks):
    tokens, width = x.shape[-2:]
    hidden = weights[0].shape[1]
    rows = tokens // 2

    def half(a, which):
        if a.ndim == 2:
            return pl.BlockSpec((tokens, width), lambda i: (0, 0))
        return pl.BlockSpec((None, tokens, width), lambda i: (which, 0, 0))

    whole = [pl.BlockSpec(w.shape, lambda i: (0, 0)) for w in weights]
    operands, specs, alias = [x, c, *weights], [half(x, 0), half(c, 1), *whole], {}
    if held is not None:
        operands.append(held)
        specs.append(pl.BlockSpec(memory_space=pl.ANY))
        alias = {5: 0}
    coded = SUMS * rows + SCALES
    return pl.pallas_call(
        functools.partial(forward_kernel, rows),
        out_shape=jax.ShapeDtypeStruct((2, chunks, coded, hidden), I16),
        grid=(1,),
        in_specs=specs,
        out_specs=pl.BlockSpec((2, None, coded, hidden), lambda i: (0, chunk, 0, 0)),
        input_output_aliases=alias,
        compiler_params=PARAMS,
        cost_estimate=cost(6 * tokens * width * hidden, 4 * tokens * width + 6 * width * hidden),
        name="forward_chunk",
    )(*operands)


def core_sum_kernel(rows, in_ref, out_ref):
    both = [decode(in_ref[i], rows) for i in range(2)]
    put(out_ref, (), [a + b for a, b in zip(*both)], rows)


def core_sum(arrived, rows):
    _, chunks, coded, hidden = arrived.shape
    return pl.pallas_call(
        functools.partial(core_sum_kernel, rows),
        out_shape=jax.ShapeDtypeStruct((chunks, coded, hidden), I16),
        grid=(chunks,),
        in_specs=[pl.BlockSpec((2, None, coded, hidden), lambda i: (0, i, 0, 0))],
        out_specs=pl.BlockSpec((None, coded, hidden), lambda i: (i, 0, 0)),
        compiler_params=PARAMS,
        cost_estimate=cost(0, 6 * chunks * coded * hidden),
        name="core_sum",
    )(arrived)


def pointwise_kernel(rows, in_ref, keep_ref, both_ref, kept_ref):
    parts = [decode(in_ref[i], rows) for i in range(in_ref.shape[0])]
    gate_pre, up_pre, grad_hidden = (sum(p[1:], p[0]) for p in zip(*parts))
    hidden = gate_pre.shape[1]
    sigmoid_gate = jax.nn.sigmoid(gate_pre)
    silu_gate = gate_pre * sigmoid_gate
    slope = sigmoid_gate * (1.0 + gate_pre * (1.0 - sigmoid_gate))
    both_ref[:, :hidden] = (grad_hidden * up_pre * slope).astype(BF16)
    both_ref[:, hidden:] = (grad_hidden * silu_gate).astype(BF16)
    kept_ref[...] = (silu_gate * up_pre * keep_ref[...]).astype(BF16)


def pointwise(arrived, keep_rows):
    rows, hidden = keep_rows.shape
    return pl.pallas_call(
        functools.partial(pointwise_kernel, rows),
        out_shape=(
            jax.ShapeDtypeStruct((rows, 2 * hidden), BF16),
            jax.ShapeDtypeStruct((rows, hidden), BF16),
        ),
        compiler_params=PARAMS,
        cost_estimate=cost(0, 2 * arrived.size),
        name="pointwise",
    )(arrived, keep_rows)


def keep_of_rows(keep_mask, rows, nz, nx, own_tokens, total):
    tiles, blocks = keep_mask.shape
    chunk = lax.axis_index("y")
    place = lax.axis_index("c") * rows + lax.broadcasted_iota(jnp.int32, (rows, 1), 0)
    rest = place - 8 * nz
    z = jnp.where(rest < 0, place // 8, rest // 4)
    inside = jnp.where(rest < 0, place % 8, 8 + rest % 4)
    shift = jnp.where(chunk == 1, -1, jnp.where(chunk == 2, 1, jnp.where(chunk == 3, 2, 0)))
    token = (z * nx + (lax.axis_index("x") + shift + nx) % nx) * own_tokens + inside
    tile = token // (total // tiles)
    chosen = tile == lax.broadcasted_iota(jnp.int32, (rows, tiles), 1)
    keep = [
        jnp.sum(jnp.where(chosen, keep_mask[:, b][None, :], 0), axis=1, keepdims=True)
        for b in range(blocks)
    ]
    return jnp.concatenate([jnp.broadcast_to(k, (rows, 128)) for k in keep], axis=1).astype(F32)


def input_grad_kernel(order, g_ref, w_ref, out_ref):
    g = g_ref[...].reshape(out_ref.shape[0], w_ref.shape[0])
    out_ref[...] = dot(g, w_ref[...], PLAIN).astype(out_ref.dtype)


def input_grad(both, weights, chunks):
    parts, rows, depth = both.shape
    width = weights.shape[1]
    tokens = parts * rows // chunks
    x = lax.axis_index("x")
    away = (jnp.arange(chunks) - x + chunks) % chunks
    order = jnp.where(away == 0, 0, jnp.where(away == 1, 2, jnp.where(away == 2, 3, 1)))
    return pl.pallas_call(
        input_grad_kernel,
        out_shape=jax.ShapeDtypeStruct((chunks, tokens, width), BF16),
        grid_spec=pltpu.PrefetchScalarGridSpec(
            num_scalar_prefetch=1,
            grid=(chunks,),
            in_specs=[
                pl.BlockSpec((parts // chunks, rows, depth), lambda d, order: (order[d], 0, 0)),
                pl.BlockSpec((depth, width), lambda d, order: (0, 0)),
            ],
            out_specs=pl.BlockSpec((None, tokens, width), lambda d, order: (d, 0, 0)),
        ),
        compiler_params=PARAMS,
        cost_estimate=cost(2 * chunks * tokens * width * depth, 2 * depth * width),
        name="input_grad",
    )(order.astype(jnp.int32), both, weights)


def x_sum_kernel(in_ref, out_ref):
    blocks = out_ref.shape[0]
    width = in_ref.shape[2]
    half = width // 2
    for first in range(0, blocks, 4):
        main = pl.ds(first * 8, 32)
        rest = pl.ds(blocks * 8 + first * 4, 16)
        main, rest = (
            sum((in_ref[i, rows].astype(F32) for i in range(1, in_ref.shape[0])), in_ref[0, rows].astype(F32))
            for rows in (main, rest)
        )
        for i in range(4):
            tail = rest[4 * i : 4 * i + 4]
            tail = jnp.concatenate([tail[:, :half], tail[:, half:]])
            block = jnp.concatenate([main[8 * i : 8 * i + 8], tail], axis=1)
            out_ref[first + i] = block.astype(BF16)


def x_sum(arrived, nz):
    width = arrived.shape[2]
    return pl.pallas_call(
        x_sum_kernel,
        out_shape=jax.ShapeDtypeStruct((nz, 8, 3 * width // 2), BF16),
        compiler_params=PARAMS,
        cost_estimate=cost(0, 2 * arrived.size),
        name="x_sum",
    )(arrived)


def z_sum_kernel(in_ref, out_ref):
    width = out_ref.shape[1]
    total = in_ref[0].astype(F32)
    for i in range(1, in_ref.shape[0]):
        total = total + in_ref[i].astype(F32)
    tail = jnp.concatenate([total[:4, width:], total[4:, width:]], axis=1)
    out_ref[...] = jnp.concatenate([total[:, :width], tail]).astype(BF16)


def z_sum(arrived, own_tokens, width):
    return pl.pallas_call(
        z_sum_kernel,
        out_shape=jax.ShapeDtypeStruct((own_tokens, width), BF16),
        compiler_params=PARAMS,
        cost_estimate=cost(0, 2 * arrived.size),
        name="z_sum",
    )(arrived)


def shards(inputs, cotangent, w_gate, w_up, w_down, keep_mask):
    own_tokens, width = inputs.shape
    hidden = w_gate.shape[1]
    nz, nx, nc = 16, 4, 2
    total = own_tokens * nz * nx
    tokens = own_tokens * nz
    rows = tokens // nc
    weights = (w_gate, w_up, w_down)

    packed = jnp.concatenate([pack(inputs), pack(cotangent)])
    along_z = lax.all_gather(packed, "z")
    own = pl.pallas_call(
        unpack_kernel,
        out_shape=jax.ShapeDtypeStruct((2, tokens, width), BF16),
        compiler_params=PARAMS,
        cost_estimate=cost(0, 8 * tokens * width),
        name="unpack",
    )(along_z)
    right = lax.ppermute(own, "x", ring(nx, 1))
    left = lax.ppermute(own, "x", ring(nx, -1))
    far_in = lax.ppermute(right[0], "x", ring(nx, 1))
    far_cot = lax.ppermute(left[1], "x", ring(nx, -1))
    own_late, w_gate_late, w_up_late = lax.optimization_barrier((own, w_gate, w_up))
    turned = jnp.concatenate([w_gate_late, w_up_late], axis=1).T

    parts = forward(0, own_late, own_late, weights, None, nx)
    parts = forward(1, right, right, weights, parts, nx)
    parts = forward(2, left, left, weights, parts, nx)
    parts = forward(3, far_in, far_cot, weights, parts, nx)

    summed = core_sum(lax.all_to_all(parts, "c", 0, 0), rows)
    keep_rows = keep_of_rows(keep_mask, rows, nz, nx, own_tokens, total)
    both, hidden_kept = pointwise(lax.all_to_all(summed, "y", 0, 0), keep_rows)
    both = lax.all_gather(both, ("y", "c"))

    result = input_grad(both, turned, nx)
    result, hidden_kept = lax.optimization_barrier((result, hidden_kept))
    arrived = lax.all_to_all(result, "x", 0, 0)
    all_kept = lax.all_gather(hidden_kept, ("y", "c")).reshape(total, hidden)
    all_inputs = jnp.concatenate([own[0], right[0], left[0], far_in])
    all_cotangent = jnp.concatenate([own[1], right[1], left[1], far_cot])
    arrived, all_kept, all_inputs, all_cotangent = lax.optimization_barrier(
        (arrived, all_kept, all_inputs, all_cotangent)
    )
    kept = x_sum(arrived, nz)
    kept, all_kept, all_inputs, all_cotangent, both = lax.optimization_barrier(
        (kept, all_kept, all_inputs, all_cotangent, both)
    )
    grad_input = z_sum(lax.all_to_all(kept, "z", 0, 0), own_tokens, width)

    both = both.reshape(total, 2 * hidden)
    grad_down = dot(all_kept, all_cotangent, OUTER).astype(BF16)
    grad_gate = dot(all_inputs, both[:, :hidden], OUTER).astype(BF16)
    grad_up = dot(all_inputs, both[:, hidden:], OUTER).astype(BF16)
    return grad_input, grad_gate, grad_up, grad_down


def solution(mesh):
    fine = Mesh(mesh.devices.reshape(16, 4, 4, 2), ("z", "x", "y", "c"))
    hid, mdl = ("z", "x"), ("y", "c")
    placed = (P(hid, mdl), P(hid, mdl), P(mdl, hid), P(mdl, hid), P(hid, mdl), P(None, hid))
    return jax.shard_map(
        shards,
        mesh=fine,
        in_specs=placed,
        out_specs=(P(hid, mdl), P(mdl, hid), P(mdl, hid), P(hid, mdl)),
        check_vma=False,
    )
```

```python
import functools

import jax
import jax.numpy as jnp
from jax import lax
from jax.experimental import pallas as pl
from jax.experimental.pallas import tpu as pltpu
from jax.sharding import Mesh, PartitionSpec as P

F32, BF16, I16 = jnp.float32, jnp.bfloat16, jnp.int16
INNER = (((1,), (1,)), ((), ()))
PLAIN = (((1,), (0,)), ((), ()))
OUTER = (((0,), (0,)), ((), ()))
SUMS = 3
SCALES = 16


def ring(size, step):
    return [(i, (i + step) % size) for i in range(size)]


def dot(a, b, dims):
    return lax.dot_general(a, b, dims, preferred_element_type=F32)


def params(mebibytes):
    return pltpu.CompilerParams(vmem_limit_bytes=mebibytes << 20)


def cost(flops, moved):
    return pl.CostEstimate(flops=flops, bytes_accessed=moved, transcendentals=0)


def row_is_lane(rows, lanes):
    shape = (rows, lanes)
    return lax.broadcasted_iota(jnp.int32, shape, 0) == lax.broadcasted_iota(jnp.int32, shape, 1)


def code(values):
    rows, lanes = values[0].shape
    diagonal = row_is_lane(rows, lanes)
    place = lax.broadcasted_iota(jnp.int32, (SCALES, lanes), 0)
    codes, tile = [], jnp.zeros((SCALES, lanes), F32)
    for k, v in enumerate(values):
        most = jnp.max(jnp.abs(v), axis=1, keepdims=True)
        exponent = jnp.ceil(jnp.log2(jnp.maximum(most, 1e-30)) + 0.01)
        codes.append(jnp.round(v * jnp.exp2(15.0 - exponent)).astype(jnp.int32).astype(I16))
        along = jnp.sum(jnp.where(diagonal, exponent, 0.0), axis=0, keepdims=True)
        tile = jnp.where(place == k, along, tile)
    return codes, tile.astype(jnp.int32).astype(I16)


def decode(block, rows):
    lanes = block.shape[1]
    diagonal = row_is_lane(rows, lanes)
    tile = jnp.exp2(block[SUMS * rows :].astype(jnp.int32).astype(F32) - 15.0)
    out = []
    for k in range(SUMS):
        scale = jnp.sum(jnp.where(diagonal, tile[k : k + 1], 0.0), axis=1, keepdims=True)
        out.append(block[k * rows : (k + 1) * rows].astype(jnp.int32).astype(F32) * scale)
    return out


def put(out_ref, index, values, rows):
    codes, tile = code(values)
    for k, c in enumerate(codes):
        out_ref[(*index, pl.ds(k * rows, rows))] = c
    out_ref[(*index, pl.ds(SUMS * rows, SCALES))] = tile


def unpack_kernel(packed_ref, *out_refs):
    blocks = packed_ref.shape[0]
    width = out_refs[0].shape[1]
    half = width // 2
    for first in range(0, blocks, 2):
        pair = [packed_ref[first + i].astype(F32) for i in range(2)]
        for which in range(2):
            part = [p[which * 8 : which * 8 + 8] for p in pair]
            out_refs[which][first * 8 : first * 8 + 16] = jnp.concatenate(
                [p[:, :width] for p in part]
            ).astype(BF16)
    for first in range(0, blocks, 4):
        four = [packed_ref[first + i, :, width:].astype(F32) for i in range(4)]
        for which in range(2):
            part = [p[which * 8 : which * 8 + 8] for p in four]
            rows = jnp.concatenate(
                [
                    jnp.concatenate([p[:4] for p in part]),
                    jnp.concatenate([p[4:] for p in part]),
                ],
                axis=1,
            )
            place = blocks * 8 + first * 4
            out_refs[which][place : place + 16] = rows.astype(BF16)


def pack_kernel(*refs):
    packed = []
    for ref in refs[:-1]:
        a = ref[...].astype(F32)
        half = a.shape[1] // 2
        tail = jnp.concatenate([a[8:, :half], a[8:, half:]])
        packed.append(jnp.concatenate([a[:8], tail], axis=1))
    refs[-1][...] = jnp.concatenate(packed).astype(BF16)


def pack(*arrays):
    width = arrays[0].shape[1]
    return pl.pallas_call(
        pack_kernel,
        out_shape=jax.ShapeDtypeStruct((8 * len(arrays), 3 * width // 2), BF16),
        cost_estimate=cost(0, 48 * len(arrays) * width),
        compiler_params=params(2),
        name="pack",
    )(*arrays)


def forward_kernel(rows, x_ref, c_ref, wg_ref, wu_ref, wd_ref, *rest):
    out_ref = rest[-1]
    x, c = x_ref[...], c_ref[...]
    values = [
        dot(x, wg_ref[...], PLAIN),
        dot(x, wu_ref[...], PLAIN),
        dot(c, wd_ref[...], INNER),
    ]
    for core in range(2):
        put(out_ref, (core,), [v[core * rows : (core + 1) * rows] for v in values], rows)


def forward(chunk, x, c, weights, held, chunks):
    tokens, width = x.shape[-2:]
    hidden = weights[0].shape[1]
    rows = tokens // 2

    half = pl.BlockSpec((tokens, width), lambda i: (0, 0))
    whole = [pl.BlockSpec(w.shape, lambda i: (0, 0)) for w in weights]
    operands, specs, alias = [x, c, *weights], [half, half, *whole], {}
    if held is not None:
        operands.append(held)
        specs.append(pl.BlockSpec(memory_space=pl.ANY))
        alias = {5: 0}
    coded = SUMS * rows + SCALES
    return pl.pallas_call(
        functools.partial(forward_kernel, rows),
        out_shape=jax.ShapeDtypeStruct((2, chunks, coded, hidden), I16),
        grid=(1,),
        in_specs=specs,
        out_specs=pl.BlockSpec((2, None, coded, hidden), lambda i: (0, chunk, 0, 0)),
        input_output_aliases=alias,
        cost_estimate=cost(6 * tokens * width * hidden, 4 * tokens * width + 6 * width * hidden),
        compiler_params=params(9),
        name="forward_chunk",
    )(*operands)


def core_sum_kernel(rows, in_ref, out_ref):
    for chunk in range(in_ref.shape[1]):
        both = [decode(in_ref[i, chunk], rows) for i in range(2)]
        put(out_ref, (chunk,), [a + b for a, b in zip(*both)], rows)


def core_sum(arrived, rows):
    return pl.pallas_call(
        functools.partial(core_sum_kernel, rows),
        out_shape=jax.ShapeDtypeStruct(arrived.shape[1:], I16),
        cost_estimate=cost(0, 3 * arrived.size),
        compiler_params=params(5),
        name="core_sum",
    )(arrived)


def pointwise_kernel(rows, in_ref, keep_ref, both_ref, kept_ref):
    parts = [decode(in_ref[i], rows) for i in range(in_ref.shape[0])]
    gate_pre, up_pre, grad_hidden = (sum(p[1:], p[0]) for p in zip(*parts))
    hidden = gate_pre.shape[1]
    sigmoid_gate = jax.nn.sigmoid(gate_pre)
    silu_gate = gate_pre * sigmoid_gate
    slope = sigmoid_gate * (1.0 + gate_pre * (1.0 - sigmoid_gate))
    both_ref[:, :hidden] = (grad_hidden * up_pre * slope).astype(BF16)
    both_ref[:, hidden:] = (grad_hidden * silu_gate).astype(BF16)
    kept_ref[...] = (silu_gate * up_pre * keep_ref[...]).astype(BF16)


def pointwise(arrived, keep_rows):
    rows, hidden = keep_rows.shape
    return pl.pallas_call(
        functools.partial(pointwise_kernel, rows),
        out_shape=(
            jax.ShapeDtypeStruct((rows, 2 * hidden), BF16),
            jax.ShapeDtypeStruct((rows, hidden), BF16),
        ),
        cost_estimate=cost(0, 2 * arrived.size),
        compiler_params=params(4),
        name="pointwise",
    )(arrived, keep_rows)


def keep_of_rows(keep_mask, rows, nz, nx, own_tokens, total):
    tiles, blocks = keep_mask.shape
    chunk = lax.axis_index("y")
    place = lax.axis_index("c") * rows + lax.broadcasted_iota(jnp.int32, (rows, 1), 0)
    rest = place - 8 * nz
    z = jnp.where(rest < 0, place // 8, rest // 4)
    inside = jnp.where(rest < 0, place % 8, 8 + rest % 4)
    shift = jnp.where(chunk == 1, -1, jnp.where(chunk == 2, 1, jnp.where(chunk == 3, 2, 0)))
    token = (z * nx + (lax.axis_index("x") + shift + nx) % nx) * own_tokens + inside
    tile = token // (total // tiles)
    chosen = tile == lax.broadcasted_iota(jnp.int32, (rows, tiles), 1)
    keep = [
        jnp.sum(jnp.where(chosen, keep_mask[:, b][None, :], 0), axis=1, keepdims=True)
        for b in range(blocks)
    ]
    return jnp.concatenate([jnp.broadcast_to(k, (rows, 128)) for k in keep], axis=1).astype(F32)


def input_grad_kernel(chunks, g_ref, wg_ref, wu_ref, out_ref):
    parts, rows, depth = g_ref.shape
    width, hidden = wg_ref.shape
    tokens = parts * rows // chunks
    g = g_ref[...].reshape(parts * rows, depth)
    x = lax.axis_index("x")
    for first in range(0, width, 256):
        columns = slice(first, first + 256)
        product = dot(g[:, :hidden], wg_ref[columns], INNER)
        product = (product + dot(g[:, hidden:], wu_ref[columns], INNER)).astype(BF16)
        for k, away in enumerate((0, -1, 1, 2)):
            owner = lax.rem(x + (away + chunks), chunks)
            out_ref[owner, :, columns] = product[k * tokens : (k + 1) * tokens]


def input_grad(both, w_gate, w_up, chunks):
    parts, rows, depth = both.shape
    width = w_gate.shape[0]
    tokens = parts * rows // chunks
    return pl.pallas_call(
        functools.partial(input_grad_kernel, chunks),
        out_shape=jax.ShapeDtypeStruct((chunks, tokens, width), BF16),
        compiler_params=params(8),
        cost_estimate=cost(2 * chunks * tokens * width * depth, 2 * depth * width),
        name="input_grad",
    )(both, w_gate, w_up)


def x_sum_kernel(in_ref, out_ref):
    blocks = out_ref.shape[0]
    width = in_ref.shape[2]
    half = width // 2
    for first in range(0, blocks, 4):
        main = pl.ds(first * 8, 32)
        rest = pl.ds(blocks * 8 + first * 4, 16)
        main, rest = (
            sum((in_ref[i, rows].astype(F32) for i in range(1, in_ref.shape[0])), in_ref[0, rows].astype(F32))
            for rows in (main, rest)
        )
        for i in range(4):
            tail = rest[4 * i : 4 * i + 4]
            tail = jnp.concatenate([tail[:, :half], tail[:, half:]])
            block = jnp.concatenate([main[8 * i : 8 * i + 8], tail], axis=1)
            out_ref[first + i] = block.astype(BF16)


def x_sum(arrived, nz):
    width = arrived.shape[2]
    return pl.pallas_call(
        x_sum_kernel,
        out_shape=jax.ShapeDtypeStruct((nz, 8, 3 * width // 2), BF16),
        cost_estimate=cost(0, 2 * arrived.size),
        compiler_params=params(5),
        name="x_sum",
    )(arrived)


def z_sum_kernel(in_ref, out_ref):
    width = out_ref.shape[1]
    total = in_ref[0].astype(F32)
    for i in range(1, in_ref.shape[0]):
        total = total + in_ref[i].astype(F32)
    tail = jnp.concatenate([total[:4, width:], total[4:, width:]], axis=1)
    out_ref[...] = jnp.concatenate([total[:, :width], tail]).astype(BF16)


def z_sum(arrived, own_tokens, width):
    return pl.pallas_call(
        z_sum_kernel,
        out_shape=jax.ShapeDtypeStruct((own_tokens, width), BF16),
        cost_estimate=cost(0, 2 * arrived.size),
        compiler_params=params(3),
        name="z_sum",
    )(arrived)


def shards(inputs, cotangent, w_gate, w_up, w_down, keep_mask):
    own_tokens, width = inputs.shape
    hidden = w_gate.shape[1]
    nz, nx, nc = 16, 4, 2
    total = own_tokens * nz * nx
    tokens = own_tokens * nz
    rows = tokens // nc
    weights = (w_gate, w_up, w_down)

    along_z = lax.all_gather(pack(inputs, cotangent), "z")
    own_in, own_cot = pl.pallas_call(
        unpack_kernel,
        out_shape=(jax.ShapeDtypeStruct((tokens, width), BF16),) * 2,
        cost_estimate=cost(0, 8 * tokens * width),
        compiler_params=params(6),
        name="unpack",
    )(along_z)
    right_in = lax.ppermute(own_in, "x", ring(nx, 1))
    left_cot = lax.ppermute(own_cot, "x", ring(nx, -1))
    right_cot = lax.ppermute(own_cot, "x", ring(nx, 1))
    left_in = lax.ppermute(own_in, "x", ring(nx, -1))
    far_in = lax.ppermute(right_in, "x", ring(nx, 1))
    far_cot = lax.ppermute(left_cot, "x", ring(nx, -1))
    parts = forward(0, own_in, own_cot, weights, None, nx)
    parts = forward(1, right_in, right_cot, weights, parts, nx)
    parts = forward(2, left_in, left_cot, weights, parts, nx)
    parts = forward(3, far_in, far_cot, weights, parts, nx)

    keep_rows = keep_of_rows(keep_mask, rows, nz, nx, own_tokens, total)
    summed = core_sum(lax.all_to_all(parts, "c", 0, 0), rows)
    summed, keep_rows = lax.optimization_barrier((summed, keep_rows))
    both, hidden_kept = pointwise(lax.all_to_all(summed, "y", 0, 0), keep_rows)
    both = lax.all_gather(both, ("y", "c"))

    arrived = lax.all_to_all(input_grad(both, w_gate, w_up, nx), "x", 0, 0)
    kept = x_sum(arrived, nz)
    blocks = (own_in, right_in, left_in, far_in, own_cot, right_cot, left_cot, far_cot)
    kept, hidden_kept, both, blocks = lax.optimization_barrier((kept, hidden_kept, both, blocks))
    grad_input = z_sum(lax.all_to_all(kept, "z", 0, 0), own_tokens, width)

    all_kept = lax.all_gather(hidden_kept, ("y", "c")).reshape(total, hidden)
    all_inputs, all_cotangent = jnp.concatenate(blocks[:nx]), jnp.concatenate(blocks[nx:])
    both = both.reshape(total, 2 * hidden)
    grad_down = dot(all_kept, all_cotangent, OUTER).astype(BF16)
    grad_gate = dot(all_inputs, both[:, :hidden], OUTER).astype(BF16)
    grad_up = dot(all_inputs, both[:, hidden:], OUTER).astype(BF16)
    return grad_input, grad_gate, grad_up, grad_down


def solution(mesh):
    fine = Mesh(mesh.devices.reshape(16, 4, 4, 2), ("z", "x", "y", "c"))
    hid, mdl = ("z", "x"), ("y", "c")
    placed = (P(hid, mdl), P(hid, mdl), P(mdl, hid), P(mdl, hid), P(hid, mdl), P(None, hid))
    return jax.shard_map(
        shards,
        mesh=fine,
        in_specs=placed,
        out_specs=(P(hid, mdl), P(mdl, hid), P(mdl, hid), P(hid, mdl)),
        check_vma=False,
    )
```

```python
import functools

import jax
import jax.numpy as jnp
from jax import lax
from jax.experimental import pallas as pl
from jax.experimental.pallas import tpu as pltpu
from jax.sharding import Mesh, PartitionSpec as P

F32, BF16, I16 = jnp.float32, jnp.bfloat16, jnp.int16
INNER = (((1,), (1,)), ((), ()))
PLAIN = (((1,), (0,)), ((), ()))
OUTER = (((0,), (0,)), ((), ()))
SUMS = 3
SCALES = 16


def ring(size, step):
    return [(i, (i + step) % size) for i in range(size)]


def dot(a, b, dims):
    return lax.dot_general(a, b, dims, preferred_element_type=F32)


def params(mebibytes):
    return pltpu.CompilerParams(vmem_limit_bytes=mebibytes << 20)


def cost(flops, moved):
    return pl.CostEstimate(flops=flops, bytes_accessed=moved, transcendentals=0)


def row_is_lane(rows, lanes):
    shape = (rows, lanes)
    return lax.broadcasted_iota(jnp.int32, shape, 0) == lax.broadcasted_iota(jnp.int32, shape, 1)


def code(values):
    rows, lanes = values[0].shape
    diagonal = row_is_lane(rows, lanes)
    place = lax.broadcasted_iota(jnp.int32, (SCALES, lanes), 0)
    codes, tile = [], jnp.zeros((SCALES, lanes), F32)
    for k, v in enumerate(values):
        most = jnp.max(jnp.abs(v), axis=1, keepdims=True)
        exponent = jnp.ceil(jnp.log2(jnp.maximum(most, 1e-30)) + 0.01)
        codes.append(jnp.round(v * jnp.exp2(15.0 - exponent)).astype(jnp.int32).astype(I16))
        along = jnp.sum(jnp.where(diagonal, exponent, 0.0), axis=0, keepdims=True)
        tile = jnp.where(place == k, along, tile)
    return codes, tile.astype(jnp.int32).astype(I16)


def decode(block, rows):
    lanes = block.shape[1]
    diagonal = row_is_lane(rows, lanes)
    tile = jnp.exp2(block[SUMS * rows :].astype(jnp.int32).astype(F32) - 15.0)
    out = []
    for k in range(SUMS):
        scale = jnp.sum(jnp.where(diagonal, tile[k : k + 1], 0.0), axis=1, keepdims=True)
        out.append(block[k * rows : (k + 1) * rows].astype(jnp.int32).astype(F32) * scale)
    return out


def put(out_ref, index, values, rows):
    codes, tile = code(values)
    for k, c in enumerate(codes):
        out_ref[(*index, pl.ds(k * rows, rows))] = c
    out_ref[(*index, pl.ds(SUMS * rows, SCALES))] = tile


def unpack_kernel(packed_ref, *out_refs):
    blocks = packed_ref.shape[0] // 2
    width = out_refs[0].shape[1]
    for odd in range(2):
        base = odd * 12 * blocks
        for first in range(0, blocks, 2):
            pair = [packed_ref[2 * (first + i) + odd].astype(F32) for i in range(2)]
            for which in range(2):
                rows = jnp.concatenate([p[which * 8 : which * 8 + 8, :width] for p in pair])
                place = base + first * 8
                out_refs[which][place : place + 16] = rows.astype(BF16)
        for first in range(0, blocks, 4):
            four = [packed_ref[2 * (first + i) + odd, :, width:].astype(F32) for i in range(4)]
            for which in range(2):
                part = [p[which * 8 : which * 8 + 8] for p in four]
                halves = [jnp.concatenate([p[h : h + 4] for p in part]) for h in (0, 4)]
                place = base + 8 * blocks + first * 4
                out_refs[which][place : place + 16] = jnp.concatenate(halves, axis=1).astype(BF16)


def pack_kernel(*refs):
    packed = []
    for ref in refs[:-1]:
        a = ref[...].astype(F32)
        half = a.shape[1] // 2
        tail = jnp.concatenate([a[8:, :half], a[8:, half:]])
        packed.append(jnp.concatenate([a[:8], tail], axis=1))
    refs[-1][...] = jnp.concatenate(packed).astype(BF16)


def pack(*arrays):
    width = arrays[0].shape[1]
    return pl.pallas_call(
        pack_kernel,
        out_shape=jax.ShapeDtypeStruct((8 * len(arrays), 3 * width // 2), BF16),
        cost_estimate=cost(0, 48 * len(arrays) * width),
        compiler_params=params(2),
        name="pack",
    )(*arrays)


def forward_kernel(rows, x_ref, c_ref, wg_ref, wu_ref, wd_ref, *rest):
    out_ref = rest[-1]
    x, c = x_ref[...], c_ref[...]
    values = [
        dot(x, wg_ref[...], PLAIN),
        dot(x, wu_ref[...], PLAIN),
        dot(c, wd_ref[...], INNER),
    ]
    for core in range(2):
        put(out_ref, (core,), [v[core * rows : (core + 1) * rows] for v in values], rows)


def forward(chunk, x, c, weights, held, chunks):
    tokens, width = x.shape[-2:]
    hidden = weights[0].shape[1]
    rows = tokens // 2

    half = pl.BlockSpec((tokens, width), lambda i: (0, 0))
    whole = [pl.BlockSpec(w.shape, lambda i: (0, 0)) for w in weights]
    operands, specs, alias = [x, c, *weights], [half, half, *whole], {}
    if held is not None:
        operands.append(held)
        specs.append(pl.BlockSpec(memory_space=pl.ANY))
        alias = {5: 0}
    coded = SUMS * rows + SCALES
    return pl.pallas_call(
        functools.partial(forward_kernel, rows),
        out_shape=jax.ShapeDtypeStruct((2, chunks, coded, hidden), I16),
        grid=(1,),
        in_specs=specs,
        out_specs=pl.BlockSpec((2, None, coded, hidden), lambda i: (0, chunk, 0, 0)),
        input_output_aliases=alias,
        cost_estimate=cost(6 * tokens * width * hidden, 4 * tokens * width + 6 * width * hidden),
        compiler_params=params(9),
        name="forward_chunk",
    )(*operands)


def core_sum_kernel(rows, in_ref, out_ref):
    for chunk in range(in_ref.shape[1]):
        both = [decode(in_ref[i, chunk], rows) for i in range(2)]
        put(out_ref, (chunk,), [a + b for a, b in zip(*both)], rows)


def core_sum(arrived, rows):
    return pl.pallas_call(
        functools.partial(core_sum_kernel, rows),
        out_shape=jax.ShapeDtypeStruct(arrived.shape[1:], I16),
        cost_estimate=cost(0, 3 * arrived.size),
        compiler_params=params(5),
        name="core_sum",
    )(arrived)


def pointwise_kernel(rows, in_ref, keep_ref, both_ref, kept_ref):
    parts = [decode(in_ref[i], rows) for i in range(in_ref.shape[0])]
    gate_pre, up_pre, grad_hidden = (sum(p[1:], p[0]) for p in zip(*parts))
    hidden = gate_pre.shape[1]
    sigmoid_gate = jax.nn.sigmoid(gate_pre)
    silu_gate = gate_pre * sigmoid_gate
    slope = sigmoid_gate * (1.0 + gate_pre * (1.0 - sigmoid_gate))
    both_ref[:, :hidden] = (grad_hidden * up_pre * slope).astype(BF16)
    both_ref[:, hidden:] = (grad_hidden * silu_gate).astype(BF16)
    kept_ref[...] = (silu_gate * up_pre * keep_ref[...]).astype(BF16)


def pointwise(arrived, keep_rows):
    rows, hidden = keep_rows.shape
    return pl.pallas_call(
        functools.partial(pointwise_kernel, rows),
        out_shape=(
            jax.ShapeDtypeStruct((rows, 2 * hidden), BF16),
            jax.ShapeDtypeStruct((rows, hidden), BF16),
        ),
        cost_estimate=cost(0, 2 * arrived.size),
        compiler_params=params(4),
        name="pointwise",
    )(arrived, keep_rows)


def keep_of_rows(keep_mask, rows, nx, own_tokens, total):
    tiles, blocks = keep_mask.shape
    chunk = lax.axis_index("y")
    place = lax.broadcasted_iota(jnp.int32, (rows, 1), 0)
    blocks_of_8 = rows // own_tokens * 8
    rest = place - blocks_of_8
    z = 2 * jnp.where(rest < 0, place // 8, rest // 4) + lax.axis_index("c")
    inside = jnp.where(rest < 0, place % 8, 8 + rest % 4)
    shift = jnp.where(chunk == 1, -1, jnp.where(chunk == 2, 1, jnp.where(chunk == 3, 2, 0)))
    token = (z * nx + (lax.axis_index("x") + shift + nx) % nx) * own_tokens + inside
    tile = token // (total // tiles)
    chosen = tile == lax.broadcasted_iota(jnp.int32, (rows, tiles), 1)
    keep = [
        jnp.sum(jnp.where(chosen, keep_mask[:, b][None, :], 0), axis=1, keepdims=True)
        for b in range(blocks)
    ]
    return jnp.concatenate([jnp.broadcast_to(k, (rows, 128)) for k in keep], axis=1).astype(F32)


def input_grad_kernel(chunks, g_ref, wg_ref, wu_ref, out_ref):
    parts, rows, depth = g_ref.shape
    width, hidden = wg_ref.shape
    tokens = parts * rows // (2 * chunks)
    g = g_ref[...].reshape(parts * rows, depth)
    x = lax.axis_index("x")
    for first in range(0, width, 256):
        columns = slice(first, first + 256)
        product = dot(g[:, :hidden], wg_ref[columns], INNER)
        product = (product + dot(g[:, hidden:], wu_ref[columns], INNER)).astype(BF16)
        for k, away in enumerate((0, -1, 1, 2)):
            owner = lax.rem(x + (away + chunks), chunks)
            for odd in range(2):
                place = (2 * k + odd) * tokens
                out_ref[odd * chunks + owner, :, columns] = product[place : place + tokens]


def input_grad(both, w_gate, w_up, chunks):
    parts, rows, depth = both.shape
    width = w_gate.shape[0]
    tokens = parts * rows // (2 * chunks)
    return pl.pallas_call(
        functools.partial(input_grad_kernel, chunks),
        out_shape=jax.ShapeDtypeStruct((2 * chunks, tokens, width), BF16),
        compiler_params=params(8),
        cost_estimate=cost(4 * chunks * tokens * width * depth, 2 * depth * width),
        name="input_grad",
    )(both, w_gate, w_up)


def x_sum_kernel(in_ref, out_ref):
    blocks = out_ref.shape[0]
    width = in_ref.shape[2]
    half = width // 2
    for first in range(0, blocks, 4):
        main = pl.ds(first * 8, 32)
        rest = pl.ds(blocks * 8 + first * 4, 16)
        main, rest = (
            sum((in_ref[i, rows].astype(F32) for i in range(1, in_ref.shape[0])), in_ref[0, rows].astype(F32))
            for rows in (main, rest)
        )
        for i in range(4):
            tail = rest[4 * i : 4 * i + 4]
            tail = jnp.concatenate([tail[:, :half], tail[:, half:]])
            block = jnp.concatenate([main[8 * i : 8 * i + 8], tail], axis=1)
            out_ref[first + i] = block.astype(BF16)


def x_sum(arrived, blocks):
    width = arrived.shape[2]
    return pl.pallas_call(
        x_sum_kernel,
        out_shape=jax.ShapeDtypeStruct((blocks, 8, 3 * width // 2), BF16),
        cost_estimate=cost(0, 2 * arrived.size),
        compiler_params=params(5),
        name="x_sum",
    )(arrived)


def z_sum_kernel(in_ref, out_ref):
    width = out_ref.shape[1]
    total = in_ref[0].astype(F32)
    for i in range(1, in_ref.shape[0]):
        total = total + in_ref[i].astype(F32)
    tail = jnp.concatenate([total[:4, width:], total[4:, width:]], axis=1)
    out_ref[...] = jnp.concatenate([total[:, :width], tail]).astype(BF16)


def z_sum(arrived, own_tokens, width):
    return pl.pallas_call(
        z_sum_kernel,
        out_shape=jax.ShapeDtypeStruct((own_tokens, width), BF16),
        cost_estimate=cost(0, 2 * arrived.size),
        compiler_params=params(3),
        name="z_sum",
    )(arrived)


def shards(inputs, cotangent, w_gate, w_up, w_down, keep_mask):
    own_tokens, width = inputs.shape
    hidden = w_gate.shape[1]
    nz, nx, nc = 16, 4, 2
    total = own_tokens * nz * nx
    tokens = own_tokens * nz
    rows = tokens // nc
    weights = (w_gate, w_up, w_down)

    along_z = lax.all_gather(pack(inputs, cotangent), ("zq", "zb"))
    own_in, own_cot = pl.pallas_call(
        unpack_kernel,
        out_shape=(jax.ShapeDtypeStruct((tokens, width), BF16),) * 2,
        cost_estimate=cost(0, 8 * tokens * width),
        compiler_params=params(6),
        name="unpack",
    )(along_z)
    right_in = lax.ppermute(own_in, "x", ring(nx, 1))
    left_cot = lax.ppermute(own_cot, "x", ring(nx, -1))
    right_cot = lax.ppermute(own_cot, "x", ring(nx, 1))
    left_in = lax.ppermute(own_in, "x", ring(nx, -1))
    far_in = lax.ppermute(right_in, "x", ring(nx, 1))
    far_cot = lax.ppermute(left_cot, "x", ring(nx, -1))
    parts = forward(0, own_in, own_cot, weights, None, nx)
    parts = forward(1, right_in, right_cot, weights, parts, nx)
    parts = forward(2, left_in, left_cot, weights, parts, nx)
    parts = forward(3, far_in, far_cot, weights, parts, nx)

    keep_rows = keep_of_rows(keep_mask, rows, nx, own_tokens, total)
    summed = core_sum(lax.all_to_all(parts, "c", 0, 0), rows)
    summed, keep_rows = lax.optimization_barrier((summed, keep_rows))
    both, hidden_kept = pointwise(lax.all_to_all(summed, "y", 0, 0), keep_rows)
    both = lax.all_gather(both, ("y", "c"))

    result = input_grad(both, w_gate, w_up, nx)
    xs, cs = (own_in, right_in, left_in, far_in), (own_cot, right_cot, left_cot, far_cot)
    result, hidden_kept, both, xs = lax.optimization_barrier((result, hidden_kept, both, xs))
    arrived = lax.all_to_all(result, ("zb", "x"), 0, 0)
    all_kept = lax.all_gather(hidden_kept, ("y", "c")).reshape(total, hidden)
    both = both.reshape(total, 2 * hidden)
    all_inputs = jnp.concatenate(xs)
    grad_gate = dot(all_inputs, both[:, :hidden], OUTER).astype(BF16)
    grad_up = dot(all_inputs, both[:, hidden:], OUTER).astype(BF16)
    arrived, all_kept, grad_gate, grad_up = lax.optimization_barrier(
        (arrived, all_kept, grad_gate, grad_up)
    )

    kept = x_sum(arrived, nz // 2)
    kept, all_kept, cs = lax.optimization_barrier((kept, all_kept, cs))
    grad_down = dot(all_kept, jnp.concatenate(cs), OUTER).astype(BF16)
    grad_input = z_sum(lax.all_to_all(kept, "zq", 0, 0), own_tokens, width)
    return grad_input, grad_gate, grad_up, grad_down


def solution(mesh):
    fine = Mesh(mesh.devices.reshape(8, 2, 4, 4, 2), ("zq", "zb", "x", "y", "c"))
    hid, mdl = ("zq", "zb", "x"), ("y", "c")
    placed = (P(hid, mdl), P(hid, mdl), P(mdl, hid), P(mdl, hid), P(hid, mdl), P(None, hid))
    return jax.shard_map(
        shards,
        mesh=fine,
        in_specs=placed,
        out_specs=(P(hid, mdl), P(mdl, hid), P(mdl, hid), P(hid, mdl)),
        check_vma=False,
    )
```

```python
import functools

import jax
import jax.numpy as jnp
from jax import lax
from jax.experimental import pallas as pl
from jax.experimental.pallas import tpu as pltpu
from jax.sharding import Mesh, PartitionSpec as P

F32, BF16, I16 = jnp.float32, jnp.bfloat16, jnp.int16
INNER = (((1,), (1,)), ((), ()))
PLAIN = (((1,), (0,)), ((), ()))
OUTER = (((0,), (0,)), ((), ()))
SUMS = 6
SCALES = 16


def ring(size, step):
    return [(i, (i + step) % size) for i in range(size)]


def dot(a, b, dims):
    return lax.dot_general(a, b, dims, preferred_element_type=F32)


def params(mebibytes):
    return pltpu.CompilerParams(vmem_limit_bytes=mebibytes << 20)


def cost(flops, moved):
    return pl.CostEstimate(flops=flops, bytes_accessed=moved, transcendentals=0)


def row_is_lane(rows, lanes):
    shape = (rows, lanes)
    return lax.broadcasted_iota(jnp.int32, shape, 0) == lax.broadcasted_iota(jnp.int32, shape, 1)


def code(values):
    rows, lanes = values[0].shape
    diagonal = row_is_lane(rows, lanes)
    place = lax.broadcasted_iota(jnp.int32, (SCALES, lanes), 0)
    codes, tile = [], jnp.zeros((SCALES, lanes), F32)
    for k, v in enumerate(values):
        most = jnp.max(jnp.abs(v), axis=1, keepdims=True)
        exponent = jnp.ceil(jnp.log2(jnp.maximum(most, 1e-30)) + 0.01)
        codes.append(jnp.round(v * jnp.exp2(15.0 - exponent)).astype(jnp.int32).astype(I16))
        along = jnp.sum(jnp.where(diagonal, exponent, 0.0), axis=0, keepdims=True)
        tile = jnp.where(place == k, along, tile)
    return codes, tile.astype(jnp.int32).astype(I16)


def decode(block, rows):
    lanes = block.shape[1]
    diagonal = row_is_lane(rows, lanes)
    tile = jnp.exp2(block[SUMS * rows :].astype(jnp.int32).astype(F32) - 15.0)
    out = []
    for k in range(SUMS):
        scale = jnp.sum(jnp.where(diagonal, tile[k : k + 1], 0.0), axis=1, keepdims=True)
        out.append(block[k * rows : (k + 1) * rows].astype(jnp.int32).astype(F32) * scale)
    return out


def put(out_ref, index, values, rows):
    codes, tile = code(values)
    for k, c in enumerate(codes):
        out_ref[(*index, pl.ds(k * rows, rows))] = c
    out_ref[(*index, pl.ds(SUMS * rows, SCALES))] = tile


def unpack_kernel(packed_ref, out_ref):
    blocks = packed_ref.shape[0] // 2
    width = out_ref.shape[2]
    for odd in range(2):
        base = odd * 12 * blocks
        for first in range(0, blocks, 2):
            pair = [packed_ref[2 * (first + i) + odd].astype(F32) for i in range(2)]
            for which in range(2):
                rows = jnp.concatenate([p[which * 8 : which * 8 + 8, :width] for p in pair])
                place = base + first * 8
                out_ref[which, place : place + 16] = rows.astype(BF16)
        for first in range(0, blocks, 4):
            four = [packed_ref[2 * (first + i) + odd, :, width:].astype(F32) for i in range(4)]
            for which in range(2):
                part = [p[which * 8 : which * 8 + 8] for p in four]
                halves = [jnp.concatenate([p[h : h + 4] for p in part]) for h in (0, 4)]
                place = base + 8 * blocks + first * 4
                out_ref[which, place : place + 16] = jnp.concatenate(halves, axis=1).astype(BF16)


def pack_kernel(*refs):
    packed = []
    for ref in refs[:-1]:
        a = ref[...].astype(F32)
        half = a.shape[1] // 2
        tail = jnp.concatenate([a[8:, :half], a[8:, half:]])
        packed.append(jnp.concatenate([a[:8], tail], axis=1))
    refs[-1][...] = jnp.concatenate(packed).astype(BF16)


def pack(*arrays):
    width = arrays[0].shape[1]
    return pl.pallas_call(
        pack_kernel,
        out_shape=jax.ShapeDtypeStruct((8 * len(arrays), 3 * width // 2), BF16),
        cost_estimate=cost(0, 48 * len(arrays) * width),
        compiler_params=params(2),
        name="pack",
    )(*arrays)


def stack_kernel(wg_ref, wu_ref, wd_ref, out_ref, sems):
    hidden, width = wd_ref.shape
    copies = [(wg_ref, out_ref.at[0]), (wu_ref, out_ref.at[1])]
    for first in range(0, width, hidden):
        part = pl.ds(first, hidden)
        copies.append((wd_ref.at[:, part], out_ref.at[2, part]))
    copies = [pltpu.make_async_copy(a, b, sems.at[i]) for i, (a, b) in enumerate(copies)]
    for c in copies:
        c.start()
    for c in copies:
        c.wait()


def stack_weights(w_gate, w_up, w_down):
    width, hidden = w_gate.shape
    spec = pl.BlockSpec(memory_space=pl.ANY)
    return pl.pallas_call(
        stack_kernel,
        out_shape=jax.ShapeDtypeStruct((3, width, hidden), BF16),
        in_specs=[spec] * 3,
        out_specs=spec,
        scratch_shapes=[pltpu.SemaphoreType.DMA((2 + width // hidden,))],
        compiler_params=params(1),
        cost_estimate=cost(0, 12 * width * hidden),
        name="stack_weights",
    )(w_gate, w_up, w_down)


def forward_kernel(rows, tokens_ref, *refs):
    out_ref = refs[-1]
    x, c = tokens_ref[0], tokens_ref[1]
    values = []
    wg_ref, wu_ref, wd_ref, pair_ref = refs[:4]
    hidden, width = wd_ref.shape
    values += [dot(x, w_ref[...], PLAIN) for w_ref in (wg_ref, wu_ref)]
    values.append(dot(c, wd_ref[...], INNER))
    values += [dot(x, pair_ref[i], PLAIN) for i in range(2)]
    blocks = [slice(first, first + hidden) for first in range(0, width, hidden)]
    products = [dot(c[:, b], pair_ref[2, b], INNER) for b in blocks]
    values.append(sum(products[1:], products[0]))
    cores, chunks = out_ref.shape[:2]
    for chunk in range(chunks):
        for core in range(cores):
            place = (chunk * cores + core) * rows
            put(out_ref, (core, chunk), [v[place : place + rows] for v in values], rows)


def forward(half, tokens, weights, held, rows, cores, chunks):
    hidden = weights[0].shape[1]
    coded = SUMS * rows + SCALES
    specs = [pl.BlockSpec(a.shape, lambda i, n=a.ndim: (0,) * n) for a in (tokens, *weights)]
    operands, alias = [tokens, *weights], {}
    if held is not None:
        operands.append(held)
        specs.append(pl.BlockSpec(memory_space=pl.ANY))
        alias = {5: 0}
    return pl.pallas_call(
        functools.partial(forward_kernel, rows),
        out_shape=jax.ShapeDtypeStruct((cores, chunks, coded, hidden), I16),
        grid=(1,),
        in_specs=specs,
        out_specs=pl.BlockSpec((cores, chunks // 2, coded, hidden), lambda i: (0, half, 0, 0)),
        input_output_aliases=alias,
        compiler_params=params(16),
        cost_estimate=cost(6 * tokens.size * hidden, 2 * tokens.size + 12 * weights[0].size),
        name="forward",
    )(*operands)


def core_sum_kernel(rows, in_ref, out_ref):
    for chunk in range(in_ref.shape[1]):
        both = [decode(in_ref[i, chunk], rows) for i in range(2)]
        put(out_ref, (chunk,), [a + b for a, b in zip(*both)], rows)


def core_sum(arrived, rows):
    return pl.pallas_call(
        functools.partial(core_sum_kernel, rows),
        out_shape=jax.ShapeDtypeStruct(arrived.shape[1:], I16),
        cost_estimate=cost(0, 3 * arrived.size),
        compiler_params=params(5),
        name="core_sum",
    )(arrived)


def pointwise_kernel(rows, in_ref, both_ref, *kept_refs):
    parts = [decode(in_ref[i], rows) for i in range(in_ref.shape[0])]
    sums = [sum(p[1:], p[0]) for p in zip(*parts)]
    hidden = sums[0].shape[1]
    for which, kept_ref in enumerate(kept_refs):
        gate_pre, up_pre, grad_hidden = sums[3 * which : 3 * which + 3]
        sigmoid_gate = jax.nn.sigmoid(gate_pre)
        silu_gate = gate_pre * sigmoid_gate
        slope = sigmoid_gate * (1.0 + gate_pre * (1.0 - sigmoid_gate))
        first = 2 * which * hidden
        both_ref[:, first : first + hidden] = (grad_hidden * up_pre * slope).astype(BF16)
        both_ref[:, first + hidden : first + 2 * hidden] = (grad_hidden * silu_gate).astype(BF16)
        kept_ref[...] = (silu_gate * up_pre).astype(BF16)


def pointwise(arrived, rows):
    hidden = arrived.shape[2]
    one = jax.ShapeDtypeStruct((rows, hidden), BF16)
    return pl.pallas_call(
        functools.partial(pointwise_kernel, rows),
        out_shape=(jax.ShapeDtypeStruct((rows, 4 * hidden), BF16), one, one),
        compiler_params=params(4),
        cost_estimate=cost(0, 2 * arrived.size),
        name="pointwise",
    )(arrived)


def pieces(refs, which, columns):
    return jnp.concatenate([r[which, :, columns] for r in refs])


def gate_up_kernel(both_ref, pair_ref, *refs):
    *tokens, gate_ref, up_ref = refs
    parts, rows, depth = both_ref.shape
    hidden = gate_ref.shape[1]
    grads = both_ref[:, :, : depth // 2].reshape(parts * rows, depth // 2)
    grads = jnp.concatenate([grads, pair_ref[...]])
    for first in range(0, gate_ref.shape[0], 256):
        columns = slice(first, first + 256)
        total = dot(pieces(tokens, 0, columns), grads, OUTER).astype(BF16)
        gate_ref[columns] = total[:, :hidden]
        up_ref[columns] = total[:, hidden:]


def gate_up_grads(both, pair, tokens):
    width, hidden = tokens[0].shape[2], pair.shape[1] // 2
    return pl.pallas_call(
        gate_up_kernel,
        out_shape=(jax.ShapeDtypeStruct((width, hidden), BF16),) * 2,
        compiler_params=params(10),
        cost_estimate=cost(16 * pair.size * width, 8 * tokens[0].size),
        name="gate_up_grads",
    )(both, pair, *tokens)


def down_kernel(kept_ref, keep_ref, *refs):
    *tokens, out_ref = refs
    rows = kept_ref.shape[1] // 2
    kept = [
        kept_ref[:, i * rows : (i + 1) * rows].reshape(keep_ref.shape[1:]) * keep_ref[i]
        for i in range(2)
    ]
    kept = jnp.concatenate(kept)
    for first in range(0, out_ref.shape[1], 256):
        columns = slice(first, first + 256)
        out_ref[:, columns] = dot(kept, pieces(tokens, 1, columns), OUTER).astype(BF16)


def down_grad(kept, keep, tokens):
    width, hidden = tokens[0].shape[2], kept.shape[2]
    return pl.pallas_call(
        down_kernel,
        out_shape=jax.ShapeDtypeStruct((hidden, width), BF16),
        compiler_params=params(9),
        cost_estimate=cost(2 * kept.size * width, 8 * tokens[0].size),
        name="down_grad",
    )(kept, keep, *tokens)


def keep_of_tokens(keep_mask, x, tokens, nx, own_tokens, total):
    tiles, blocks = keep_mask.shape
    row = lax.broadcasted_iota(jnp.int32, (tokens, 1), 0)
    per_kind = tokens // 4
    place, eights = row % per_kind, per_kind // own_tokens * 8
    rest = place - eights
    z = 2 * jnp.where(rest < 0, place // 8, rest // 4) + row // per_kind % 2
    inside = jnp.where(rest < 0, place % 8, 8 + rest % 4)
    other = row // (2 * per_kind)
    from_x = x + other * (1 - 2 * (x % 2))
    tile = ((z * nx + from_x) * own_tokens + inside) // (total // tiles)
    chosen = tile == lax.broadcasted_iota(jnp.int32, (tokens, tiles), 1)
    keep = [
        jnp.sum(jnp.where(chosen, keep_mask[:, b][None, :], 0), axis=1, keepdims=True)
        for b in range(blocks)
    ]
    return jnp.concatenate([jnp.broadcast_to(k, (tokens, 128)) for k in keep], axis=1).astype(BF16)


def input_grad_kernel(g_ref, wg_ref, wu_ref, pair_ref, out_ref):
    chunks, rows, width = out_ref.shape
    hidden = wg_ref.shape[1]
    xl = lax.axis_index("xl")
    g = g_ref[...].reshape(chunks * rows, 4 * hidden)
    for first in range(0, width, 256):
        columns = slice(first, first + 256)
        places = (wg_ref[columns], wu_ref[columns], pair_ref[0, columns], pair_ref[1, columns])
        product = dot(g[:, :hidden], places[0], INNER)
        for i, w in enumerate(places[1:], 1):
            product = product + dot(g[:, i * hidden : (i + 1) * hidden], w, INNER)
        product = product.astype(BF16)
        for k in range(2):
            owner = lax.rem(xl + k, 2)
            for odd in range(2):
                place = (2 * k + odd) * rows
                out_ref[2 * odd + owner, :, columns] = product[place : place + rows]


def input_grad(both, weights, chunks):
    parts, rows, depth = both.shape
    width = weights[0].shape[0]
    tokens = parts * rows
    return pl.pallas_call(
        input_grad_kernel,
        out_shape=jax.ShapeDtypeStruct((chunks, tokens // chunks, width), BF16),
        compiler_params=params(10),
        cost_estimate=cost(2 * tokens * width * depth, 2 * depth * width),
        name="input_grad",
    )(both, *weights)


def x_sum_kernel(in_ref, out_ref):
    blocks = out_ref.shape[0]
    width = in_ref.shape[2]
    half = width // 2
    for first in range(0, blocks, 4):
        main = pl.ds(first * 8, 32)
        rest = pl.ds(blocks * 8 + first * 4, 16)
        main, rest = (
            sum((in_ref[i, rows].astype(F32) for i in range(1, in_ref.shape[0])), in_ref[0, rows].astype(F32))
            for rows in (main, rest)
        )
        for i in range(4):
            tail = rest[4 * i : 4 * i + 4]
            tail = jnp.concatenate([tail[:, :half], tail[:, half:]])
            block = jnp.concatenate([main[8 * i : 8 * i + 8], tail], axis=1)
            out_ref[first + i] = block.astype(BF16)


def x_sum(arrived, blocks):
    width = arrived.shape[2]
    return pl.pallas_call(
        x_sum_kernel,
        out_shape=jax.ShapeDtypeStruct((blocks, 8, 3 * width // 2), BF16),
        cost_estimate=cost(0, 2 * arrived.size),
        compiler_params=params(5),
        name="x_sum",
    )(arrived)


def z_sum_kernel(in_ref, out_ref):
    width = out_ref.shape[1]
    total = in_ref[0].astype(F32)
    for i in range(1, in_ref.shape[0]):
        total = total + in_ref[i].astype(F32)
    tail = jnp.concatenate([total[:4, width:], total[4:, width:]], axis=1)
    out_ref[...] = jnp.concatenate([total[:, :width], tail]).astype(BF16)


def z_sum(arrived, own_tokens, width):
    return pl.pallas_call(
        z_sum_kernel,
        out_shape=jax.ShapeDtypeStruct((own_tokens, width), BF16),
        cost_estimate=cost(0, 2 * arrived.size),
        compiler_params=params(3),
        name="z_sum",
    )(arrived)


def shards(inputs, cotangent, w_gate, w_up, w_down, keep_mask):
    own_tokens, width = inputs.shape
    hidden = w_gate.shape[1]
    nz, nx, ny, nc = 16, 4, 4, 2
    total = own_tokens * nz * nx
    tokens = total // 2
    rows = tokens // (ny * nc)

    def to_partner(a):
        return lax.ppermute(a, ("xh", "xl"), [(0, 3), (3, 0), (1, 2), (2, 1)])

    w_2 = to_partner(stack_weights(w_gate, w_up, w_down))
    along_z = lax.all_gather(pack(inputs, cotangent), ("zq", "zb"))
    own = pl.pallas_call(
        unpack_kernel,
        out_shape=jax.ShapeDtypeStruct((2, tokens // 2, width), BF16),
        cost_estimate=cost(0, 4 * tokens * width),
        compiler_params=params(6),
        name="unpack",
    )(along_z)
    other = lax.ppermute(own, "xl", ring(2, 1))
    weights = (w_gate, w_up, w_down, w_2)

    parts = forward(0, own, weights, None, rows, nc, ny)
    parts = forward(1, other, weights, parts, rows, nc, ny)
    summed = core_sum(lax.all_to_all(parts, "c", 0, 0), rows)
    own_2 = to_partner(own)
    summed, own_2, other_late = lax.optimization_barrier((summed, own_2, other))
    other_2 = to_partner(other_late)
    both, kept, kept_2 = pointwise(lax.all_to_all(summed, "y", 0, 0), rows)
    both = lax.all_gather(both, ("y", "c"))
    both, other_2 = lax.optimization_barrier((both, other_2))

    result = input_grad(both, (w_gate, w_up, w_2), nx)
    result, both, kept, kept_2 = lax.optimization_barrier((result, both, kept, kept_2))
    arrived = lax.all_to_all(result, ("zb", "xl"), 0, 0)
    both_2 = to_partner(both.reshape(tokens, 4 * hidden)[:, 2 * hidden :])
    kept = jnp.concatenate([kept, to_partner(kept_2)])
    x = lax.axis_index(("xh", "xl"))
    keep = jnp.stack(
        [
            keep_of_tokens(keep_mask, at, tokens, nx, own_tokens, total)
            for at in (x, nx - 1 - x)
        ]
    )
    arrived, kept, keep = lax.optimization_barrier((arrived, kept, keep))

    grad_sum = x_sum(arrived, nz // 2)
    grad_sum, kept = lax.optimization_barrier((grad_sum, kept))
    grad_input = z_sum(lax.all_to_all(grad_sum, "zq", 0, 0), own_tokens, width)
    kept = lax.all_gather(kept, ("y", "c"))
    places = (own, other, own_2, other_2)
    grad_gate, grad_up = gate_up_grads(both, both_2, places)
    grad_down = down_grad(kept, keep, places)
    return grad_input, grad_gate, grad_up, grad_down


def solution(mesh):
    fine = Mesh(mesh.devices.reshape(8, 2, 2, 2, 4, 2), ("zq", "zb", "xh", "xl", "y", "c"))
    hid, mdl = ("zq", "zb", "xh", "xl"), ("y", "c")
    placed = (P(hid, mdl), P(hid, mdl), P(mdl, hid), P(mdl, hid), P(hid, mdl), P(None, hid))
    return jax.shard_map(
        shards,
        mesh=fine,
        in_specs=placed,
        out_specs=(P(hid, mdl), P(mdl, hid), P(mdl, hid), P(hid, mdl)),
        check_vma=False,
    )
```

```python
import functools

import jax
import jax.numpy as jnp
from jax import lax
from jax.experimental import pallas as pl
from jax.experimental.pallas import tpu as pltpu
from jax.sharding import Mesh, PartitionSpec as P

F32, BF16, I16 = jnp.float32, jnp.bfloat16, jnp.int16
INNER = (((1,), (1,)), ((), ()))
PLAIN = (((1,), (0,)), ((), ()))
OUTER = (((0,), (0,)), ((), ()))
SUMS = 6
SIDES = 3
SCALES = 16


def ring(size, step):
    return [(i, (i + step) % size) for i in range(size)]


def dot(a, b, dims):
    return lax.dot_general(a, b, dims, preferred_element_type=F32)


def params(mebibytes):
    return pltpu.CompilerParams(vmem_limit_bytes=mebibytes << 20)


def cost(flops, moved):
    return pl.CostEstimate(flops=flops, bytes_accessed=moved, transcendentals=0)


def row_is_lane(rows, lanes):
    shape = (rows, lanes)
    return lax.broadcasted_iota(jnp.int32, shape, 0) == lax.broadcasted_iota(jnp.int32, shape, 1)


def exponent_of(values):
    most = jnp.max(jnp.abs(values), axis=1, keepdims=True)
    return jnp.ceil(jnp.log2(jnp.maximum(most, 1e-30)) + 0.01)


def integers(values, exponent):
    return jnp.round(values * jnp.exp2(15.0 - exponent)).astype(jnp.int32).astype(I16)


def code(values):
    rows, lanes = values[0].shape
    diagonal = row_is_lane(rows, lanes)
    place = lax.broadcasted_iota(jnp.int32, (SCALES, lanes), 0)
    codes, tile = [], jnp.zeros((SCALES, lanes), F32)
    for k, v in enumerate(values):
        exponent = exponent_of(v)
        codes.append(integers(v, exponent))
        along = jnp.sum(jnp.where(diagonal, exponent, 0.0), axis=0, keepdims=True)
        tile = jnp.where(place == k, along, tile)
    return codes, tile.astype(jnp.int32).astype(I16)


def decode(block, rows):
    lanes = block.shape[1]
    diagonal = row_is_lane(rows, lanes)
    tile = jnp.exp2(block[SUMS * rows :].astype(jnp.int32).astype(F32) - 15.0)
    out = []
    for k in range(SUMS):
        scale = jnp.sum(jnp.where(diagonal, tile[k : k + 1], 0.0), axis=1, keepdims=True)
        out.append(block[k * rows : (k + 1) * rows].astype(jnp.int32).astype(F32) * scale)
    return out


def put(out_ref, index, values, rows):
    codes, tile = code(values)
    for k, c in enumerate(codes):
        out_ref[(*index, pl.ds(k * rows, rows))] = c
    out_ref[(*index, pl.ds(SUMS * rows, SCALES))] = tile


def unpack_kernel(packed_ref, out_ref):
    blocks = packed_ref.shape[0] // 2
    width = out_ref.shape[2]
    for odd in range(2):
        base = odd * 12 * blocks
        for first in range(0, blocks, 2):
            pair = [packed_ref[2 * (first + i) + odd].astype(F32) for i in range(2)]
            for which in range(2):
                rows = jnp.concatenate([p[which * 8 : which * 8 + 8, :width] for p in pair])
                place = base + first * 8
                out_ref[which, place : place + 16] = rows.astype(BF16)
        for first in range(0, blocks, 4):
            four = [packed_ref[2 * (first + i) + odd, :, width:].astype(F32) for i in range(4)]
            for which in range(2):
                part = [p[which * 8 : which * 8 + 8] for p in four]
                halves = [jnp.concatenate([p[h : h + 4] for p in part]) for h in (0, 4)]
                place = base + 8 * blocks + first * 4
                out_ref[which, place : place + 16] = jnp.concatenate(halves, axis=1).astype(BF16)


def pack_kernel(*refs):
    packed = []
    for ref in refs[:-1]:
        a = ref[...].astype(F32)
        half = a.shape[1] // 2
        tail = jnp.concatenate([a[8:, :half], a[8:, half:]])
        packed.append(jnp.concatenate([a[:8], tail], axis=1))
    refs[-1][...] = jnp.concatenate(packed).astype(BF16)


def pack(*arrays):
    width = arrays[0].shape[1]
    return pl.pallas_call(
        pack_kernel,
        out_shape=jax.ShapeDtypeStruct((8 * len(arrays), 3 * width // 2), BF16),
        cost_estimate=cost(0, 48 * len(arrays) * width),
        compiler_params=params(2),
        name="pack",
    )(*arrays)


def stack_kernel(wg_ref, wu_ref, wd_ref, out_ref, held, sems):
    hidden, width = wd_ref.shape
    copies = []
    for first in range(0, width, hidden):
        part = pl.ds(first, hidden)
        for k, source in enumerate((wg_ref.at[part], wu_ref.at[part], wd_ref.at[:, part])):
            place, sem = held.at[k, part], sems.at[len(copies)]
            copies.append(
                (
                    pltpu.make_async_copy(source, place, sem),
                    pltpu.make_async_copy(place, out_ref.at[k, part], sem),
                )
            )
    for into, _ in copies:
        into.start()
    for into, out in copies:
        into.wait()
        out.start()
    for _, out in copies:
        out.wait()


def stack_weights(w_gate, w_up, w_down):
    width, hidden = w_gate.shape
    spec = pl.BlockSpec(memory_space=pl.ANY)
    return pl.pallas_call(
        stack_kernel,
        out_shape=jax.ShapeDtypeStruct((3, width, hidden), BF16),
        in_specs=[spec] * 3,
        out_specs=spec,
        scratch_shapes=[
            pltpu.VMEM((3, width, hidden), BF16),
            pltpu.SemaphoreType.DMA((3 * (width // hidden),)),
        ],
        compiler_params=params(56),
        cost_estimate=cost(0, 12 * width * hidden),
        name="stack_weights",
    )(w_gate, w_up, w_down)


def forward_kernel(rows, tokens_ref, *refs):
    out_ref = refs[-1]
    x, c = tokens_ref[0], tokens_ref[1]
    values = []
    wg_ref, wu_ref, wd_ref, pair_ref = refs[:4]
    hidden, width = wd_ref.shape
    values += [dot(x, w_ref[...], PLAIN) for w_ref in (wg_ref, wu_ref)]
    values.append(dot(c, wd_ref[...], INNER))
    values += [dot(x, pair_ref[i], PLAIN) for i in range(2)]
    blocks = [slice(first, first + hidden) for first in range(0, width, hidden)]
    products = [dot(c[:, b], pair_ref[2, b], INNER) for b in blocks]
    values.append(sum(products[1:], products[0]))
    cores, chunks = out_ref.shape[:2]
    for chunk in range(chunks):
        for core in range(cores):
            place = (chunk * cores + core) * rows
            put(out_ref, (core, chunk), [v[place : place + rows] for v in values], rows)


def forward(half, tokens, weights, held, rows, cores, chunks):
    hidden = weights[0].shape[1]
    coded = SUMS * rows + SCALES
    specs = [pl.BlockSpec(a.shape, lambda i, n=a.ndim: (0,) * n) for a in (tokens, *weights)]
    operands, alias = [tokens, *weights], {}
    if held is not None:
        operands.append(held)
        specs.append(pl.BlockSpec(memory_space=pl.ANY))
        alias = {5: 0}
    return pl.pallas_call(
        functools.partial(forward_kernel, rows),
        out_shape=jax.ShapeDtypeStruct((cores, chunks, coded, hidden), I16),
        grid=(1,),
        in_specs=specs,
        out_specs=pl.BlockSpec((cores, chunks // 2, coded, hidden), lambda i: (0, half, 0, 0)),
        input_output_aliases=alias,
        compiler_params=params(16),
        cost_estimate=cost(6 * tokens.size * hidden, 2 * tokens.size + 12 * weights[0].size),
        name="forward",
    )(*operands)


def core_sum_kernel(rows, in_ref, out_ref):
    for chunk in range(in_ref.shape[1]):
        both = [decode(in_ref[i, chunk], rows) for i in range(2)]
        put(out_ref, (chunk,), [a + b for a, b in zip(*both)], rows)


def core_sum(arrived, rows):
    return pl.pallas_call(
        functools.partial(core_sum_kernel, rows),
        out_shape=jax.ShapeDtypeStruct(arrived.shape[1:], I16),
        cost_estimate=cost(0, 3 * arrived.size),
        compiler_params=params(5),
        name="core_sum",
    )(arrived)


def pointwise_kernel(rows, in_ref, out_ref):
    parts = [decode(in_ref[i], rows) for i in range(in_ref.shape[0])]
    sums = [sum(p[1:], p[0]) for p in zip(*parts)]
    hidden = sums[0].shape[1]
    grads, kept = [], []
    for which in range(2):
        gate_pre, up_pre, grad_hidden = sums[3 * which : 3 * which + 3]
        sigmoid_gate = jax.nn.sigmoid(gate_pre)
        silu_gate = gate_pre * sigmoid_gate
        slope = sigmoid_gate * (1.0 + gate_pre * (1.0 - sigmoid_gate))
        grads += [grad_hidden * up_pre * slope, grad_hidden * silu_gate]
        kept.append(silu_gate * up_pre)
    lane = lax.broadcasted_iota(jnp.int32, (rows, 128), 1)
    exponents = jnp.zeros((rows, 128), F32)
    for k, v in enumerate(grads + kept):
        v = v.astype(BF16).astype(F32)
        exponent = exponent_of(v)
        exponents = jnp.where(lane == k, exponent, exponents)
        out_ref[:, k * hidden : (k + 1) * hidden] = integers(v, exponent)
    out_ref[:, SUMS * hidden :] = exponents.astype(jnp.int32).astype(I16)


def pointwise(arrived, rows):
    hidden = arrived.shape[2]
    return pl.pallas_call(
        functools.partial(pointwise_kernel, rows),
        out_shape=jax.ShapeDtypeStruct((rows, SUMS * hidden + 128), I16),
        compiler_params=params(4),
        cost_estimate=cost(0, 2 * arrived.size),
        name="pointwise",
    )(arrived)


def pieces(refs, which, columns):
    return jnp.concatenate([r[which, :, columns] for r in refs])


def gate_up_kernel(own_ref, pair_ref, *refs):
    *tokens, gate_ref, up_ref = refs
    hidden = gate_ref.shape[1]
    grads = jnp.concatenate([own_ref[:, : 2 * hidden], pair_ref[:, : 2 * hidden]])
    for first in range(0, gate_ref.shape[0], 256):
        columns = slice(first, first + 256)
        total = dot(pieces(tokens, 0, columns), grads, OUTER).astype(BF16)
        gate_ref[columns] = total[:, :hidden]
        up_ref[columns] = total[:, hidden:]


def gate_up_grads(own, pair, tokens):
    width, hidden = tokens[0].shape[2], own.shape[1] // SIDES
    return pl.pallas_call(
        gate_up_kernel,
        out_shape=(jax.ShapeDtypeStruct((width, hidden), BF16),) * 2,
        compiler_params=params(10),
        cost_estimate=cost(8 * own.shape[0] * hidden * width, 8 * tokens[0].size),
        name="gate_up_grads",
    )(own, pair, *tokens)


def down_kernel(own_ref, pair_ref, keep_ref, *refs):
    *tokens, out_ref = refs
    hidden = out_ref.shape[0]
    kept = [ref[:, 2 * hidden :] * keep_ref[i] for i, ref in enumerate((own_ref, pair_ref))]
    kept = jnp.concatenate(kept)
    for first in range(0, out_ref.shape[1], 256):
        columns = slice(first, first + 256)
        out_ref[:, columns] = dot(kept, pieces(tokens, 1, columns), OUTER).astype(BF16)


def down_grad(own, pair, keep, tokens):
    width, hidden = tokens[0].shape[2], own.shape[1] // SIDES
    return pl.pallas_call(
        down_kernel,
        out_shape=jax.ShapeDtypeStruct((hidden, width), BF16),
        compiler_params=params(9),
        cost_estimate=cost(4 * own.shape[0] * hidden * width, 8 * tokens[0].size),
        name="down_grad",
    )(own, pair, keep, *tokens)


def keep_of_tokens(keep_mask, x, tokens, nx, own_tokens, total):
    tiles, blocks = keep_mask.shape
    row = lax.broadcasted_iota(jnp.int32, (tokens, 1), 0)
    per_kind = tokens // 4
    place, eights = row % per_kind, per_kind // own_tokens * 8
    rest = place - eights
    z = 2 * jnp.where(rest < 0, place // 8, rest // 4) + row // per_kind % 2
    inside = jnp.where(rest < 0, place % 8, 8 + rest % 4)
    other = row // (2 * per_kind)
    from_x = x + other * (1 - 2 * (x % 2))
    tile = ((z * nx + from_x) * own_tokens + inside) // (total // tiles)
    chosen = tile == lax.broadcasted_iota(jnp.int32, (tokens, tiles), 1)
    keep = [
        jnp.sum(jnp.where(chosen, keep_mask[:, b][None, :], 0), axis=1, keepdims=True)
        for b in range(blocks)
    ]
    return jnp.concatenate([jnp.broadcast_to(k, (tokens, 128)) for k in keep], axis=1).astype(BF16)


def gathered_values(coded_ref, hidden, wanted):
    coded = coded_ref[...].reshape(coded_ref.shape[0] * coded_ref.shape[1], coded_ref.shape[2])
    scales = jnp.exp2(coded[:, SUMS * hidden :].astype(jnp.int32).astype(F32) - 15.0)
    values = []
    for k in wanted:
        v = coded[:, k * hidden : (k + 1) * hidden].astype(jnp.int32).astype(F32)
        values.append((v * scales[:, k : k + 1]).astype(BF16))
    return values


def sides_kernel(coded_ref, *side_refs):
    for which, side_ref in enumerate(side_refs):
        hidden = side_ref.shape[1] // SIDES
        values = gathered_values(coded_ref, hidden, (2 * which, 2 * which + 1, 4 + which))
        for i, v in enumerate(values):
            side_ref[:, i * hidden : (i + 1) * hidden] = v


def sides(coded, hidden):
    side = jax.ShapeDtypeStruct((coded.shape[0] * coded.shape[1], SIDES * hidden), BF16)
    return pl.pallas_call(
        sides_kernel,
        out_shape=(side, side),
        compiler_params=params(8),
        cost_estimate=cost(0, 4 * coded.size),
        name="sides",
    )(coded)


def input_grad_kernel(g_ref, wg_ref, wu_ref, pair_ref, out_ref):
    chunks, rows, width = out_ref.shape
    hidden = wg_ref.shape[1]
    xl = lax.axis_index("xl")
    g = gathered_values(g_ref, hidden, range(4))
    for first in range(0, width, 256):
        columns = slice(first, first + 256)
        places = (wg_ref[columns], wu_ref[columns], pair_ref[0, columns], pair_ref[1, columns])
        product = dot(g[0], places[0], INNER)
        for v, w in zip(g[1:], places[1:]):
            product = product + dot(v, w, INNER)
        product = product.astype(BF16)
        for k in range(2):
            owner = lax.rem(xl + k, 2)
            for odd in range(2):
                place = (2 * k + odd) * rows
                out_ref[2 * odd + owner, :, columns] = product[place : place + rows]


def input_grad(coded, weights, chunks):
    width, hidden = weights[0].shape
    tokens = coded.shape[0] * coded.shape[1]
    return pl.pallas_call(
        input_grad_kernel,
        out_shape=jax.ShapeDtypeStruct((chunks, tokens // chunks, width), BF16),
        compiler_params=params(12),
        cost_estimate=cost(8 * tokens * width * hidden, 2 * coded.size),
        name="input_grad",
    )(coded, *weights)


def x_sum_kernel(in_ref, out_ref):
    blocks = out_ref.shape[0]
    width = in_ref.shape[2]
    half = width // 2
    for first in range(0, blocks, 4):
        main = pl.ds(first * 8, 32)
        rest = pl.ds(blocks * 8 + first * 4, 16)
        main, rest = (
            sum((in_ref[i, rows].astype(F32) for i in range(1, in_ref.shape[0])), in_ref[0, rows].astype(F32))
            for rows in (main, rest)
        )
        for i in range(4):
            tail = rest[4 * i : 4 * i + 4]
            tail = jnp.concatenate([tail[:, :half], tail[:, half:]])
            block = jnp.concatenate([main[8 * i : 8 * i + 8], tail], axis=1)
            out_ref[first + i] = block.astype(BF16)


def x_sum(arrived, blocks):
    width = arrived.shape[2]
    return pl.pallas_call(
        x_sum_kernel,
        out_shape=jax.ShapeDtypeStruct((blocks, 8, 3 * width // 2), BF16),
        cost_estimate=cost(0, 2 * arrived.size),
        compiler_params=params(5),
        name="x_sum",
    )(arrived)


def z_sum_kernel(in_ref, out_ref):
    width = out_ref.shape[1]
    total = in_ref[0].astype(F32)
    for i in range(1, in_ref.shape[0]):
        total = total + in_ref[i].astype(F32)
    tail = jnp.concatenate([total[:4, width:], total[4:, width:]], axis=1)
    out_ref[...] = jnp.concatenate([total[:, :width], tail]).astype(BF16)


def z_sum(arrived, own_tokens, width):
    return pl.pallas_call(
        z_sum_kernel,
        out_shape=jax.ShapeDtypeStruct((own_tokens, width), BF16),
        cost_estimate=cost(0, 2 * arrived.size),
        compiler_params=params(3),
        name="z_sum",
    )(arrived)


def shards(inputs, cotangent, w_gate, w_up, w_down, keep_mask):
    own_tokens, width = inputs.shape
    hidden = w_gate.shape[1]
    nz, nx, ny, nc = 16, 4, 4, 2
    total = own_tokens * nz * nx
    tokens = total // 2
    rows = tokens // (ny * nc)

    def to_partner(a):
        return lax.ppermute(a, ("xh", "xl"), [(0, 3), (3, 0), (1, 2), (2, 1)])

    w_2 = to_partner(stack_weights(w_gate, w_up, w_down))
    along_z = lax.all_gather(pack(inputs, cotangent), ("zq", "zb"))
    own = pl.pallas_call(
        unpack_kernel,
        out_shape=jax.ShapeDtypeStruct((2, tokens // 2, width), BF16),
        cost_estimate=cost(0, 4 * tokens * width),
        compiler_params=params(6),
        name="unpack",
    )(along_z)
    other = lax.ppermute(own, "xl", ring(2, 1))
    weights = (w_gate, w_up, w_down, w_2)

    parts = forward(0, own, weights, None, rows, nc, ny)
    parts = forward(1, other, weights, parts, rows, nc, ny)
    summed = core_sum(lax.all_to_all(parts, "c", 0, 0), rows)
    own_2 = to_partner(own)
    summed, own_2, other_late = lax.optimization_barrier((summed, own_2, other))
    other_2 = to_partner(other_late)
    coded = lax.all_gather(pointwise(lax.all_to_all(summed, "y", 0, 0), rows), ("y", "c"))
    coded, other_2 = lax.optimization_barrier((coded, other_2))

    result = input_grad(coded, (w_gate, w_up, w_2), nx)
    result, coded = lax.optimization_barrier((result, coded))
    arrived = lax.all_to_all(result, ("zb", "xl"), 0, 0)
    mine, pair = sides(coded, hidden)
    pair = to_partner(pair)
    x = lax.axis_index(("xh", "xl"))
    keep = jnp.stack(
        [
            keep_of_tokens(keep_mask, at, tokens, nx, own_tokens, total)
            for at in (x, nx - 1 - x)
        ]
    )
    arrived, keep = lax.optimization_barrier((arrived, keep))

    grad_sum = x_sum(arrived, nz // 2)
    grad_input = z_sum(lax.all_to_all(grad_sum, "zq", 0, 0), own_tokens, width)
    places = (own, other, own_2, other_2)
    grad_gate, grad_up = gate_up_grads(mine, pair, places)
    grad_down = down_grad(mine, pair, keep, places)
    return grad_input, grad_gate, grad_up, grad_down


def solution(mesh):
    fine = Mesh(mesh.devices.reshape(8, 2, 2, 2, 4, 2), ("zq", "zb", "xh", "xl", "y", "c"))
    hid, mdl = ("zq", "zb", "xh", "xl"), ("y", "c")
    placed = (P(hid, mdl), P(hid, mdl), P(mdl, hid), P(mdl, hid), P(hid, mdl), P(None, hid))
    return jax.shard_map(
        shards,
        mesh=fine,
        in_specs=placed,
        out_specs=(P(hid, mdl), P(mdl, hid), P(mdl, hid), P(hid, mdl)),
        check_vma=False,
    )
```

```python
import functools

import jax
import jax.numpy as jnp
from jax import lax
from jax.experimental import pallas as pl
from jax.experimental.pallas import tpu as pltpu
from jax.sharding import Mesh, PartitionSpec as P

F32, BF16, I16 = jnp.float32, jnp.bfloat16, jnp.int16
INNER = (((1,), (1,)), ((), ()))
PLAIN = (((1,), (0,)), ((), ()))
OUTER = (((0,), (0,)), ((), ()))
SUMS = 6
SIDES = 3
SCALES = 16


def ring(size, step):
    return [(i, (i + step) % size) for i in range(size)]


def dot(a, b, dims):
    return lax.dot_general(a, b, dims, preferred_element_type=F32)


def params(mebibytes):
    return pltpu.CompilerParams(vmem_limit_bytes=mebibytes << 20)


def cost(flops, moved):
    return pl.CostEstimate(flops=flops, bytes_accessed=moved, transcendentals=0)


def row_is_lane(rows, lanes):
    shape = (rows, lanes)
    return lax.broadcasted_iota(jnp.int32, shape, 0) == lax.broadcasted_iota(jnp.int32, shape, 1)


def exponent_of(values):
    most = jnp.max(jnp.abs(values), axis=1, keepdims=True)
    return jnp.ceil(jnp.log2(jnp.maximum(most, 1e-30)) + 0.01)


def integers(values, exponent):
    return jnp.round(values * jnp.exp2(15.0 - exponent)).astype(jnp.int32).astype(I16)


def code(values):
    rows, lanes = values[0].shape
    diagonal = row_is_lane(rows, lanes)
    place = lax.broadcasted_iota(jnp.int32, (SCALES, lanes), 0)
    codes, tile = [], jnp.zeros((SCALES, lanes), F32)
    for k, v in enumerate(values):
        exponent = exponent_of(v)
        codes.append(integers(v, exponent))
        along = jnp.sum(jnp.where(diagonal, exponent, 0.0), axis=0, keepdims=True)
        tile = jnp.where(place == k, along, tile)
    return codes, tile.astype(jnp.int32).astype(I16)


def decode(block, rows):
    lanes = block.shape[1]
    diagonal = row_is_lane(rows, lanes)
    tile = jnp.exp2(block[SUMS * rows :].astype(jnp.int32).astype(F32) - 15.0)
    out = []
    for k in range(SUMS):
        scale = jnp.sum(jnp.where(diagonal, tile[k : k + 1], 0.0), axis=1, keepdims=True)
        out.append(block[k * rows : (k + 1) * rows].astype(jnp.int32).astype(F32) * scale)
    return out


def put(out_ref, index, values, rows):
    codes, tile = code(values)
    for k, c in enumerate(codes):
        out_ref[(*index, pl.ds(k * rows, rows))] = c
    out_ref[(*index, pl.ds(SUMS * rows, SCALES))] = tile


def unpack_kernel(packed_ref, out_ref):
    blocks = packed_ref.shape[0] // 2
    width = out_ref.shape[2]
    for odd in range(2):
        base = odd * 12 * blocks
        for first in range(0, blocks, 2):
            pair = [packed_ref[2 * (first + i) + odd].astype(F32) for i in range(2)]
            for which in range(2):
                rows = jnp.concatenate([p[which * 8 : which * 8 + 8, :width] for p in pair])
                place = base + first * 8
                out_ref[which, place : place + 16] = rows.astype(BF16)
        for first in range(0, blocks, 4):
            four = [packed_ref[2 * (first + i) + odd, :, width:].astype(F32) for i in range(4)]
            for which in range(2):
                part = [p[which * 8 : which * 8 + 8] for p in four]
                halves = [jnp.concatenate([p[h : h + 4] for p in part]) for h in (0, 4)]
                place = base + 8 * blocks + first * 4
                out_ref[which, place : place + 16] = jnp.concatenate(halves, axis=1).astype(BF16)


def pack_kernel(*refs):
    packed = []
    for ref in refs[:-1]:
        a = ref[...].astype(F32)
        half = a.shape[1] // 2
        tail = jnp.concatenate([a[8:, :half], a[8:, half:]])
        packed.append(jnp.concatenate([a[:8], tail], axis=1))
    refs[-1][...] = jnp.concatenate(packed).astype(BF16)


def pack(*arrays):
    width = arrays[0].shape[1]
    return pl.pallas_call(
        pack_kernel,
        out_shape=jax.ShapeDtypeStruct((8 * len(arrays), 3 * width // 2), BF16),
        cost_estimate=cost(0, 48 * len(arrays) * width),
        compiler_params=params(2),
        name="pack",
    )(*arrays)


def stack_kernel(wg_ref, wu_ref, wd_ref, out_ref, held, sems):
    hidden, width = wd_ref.shape
    copies = []
    for first in range(0, width, hidden):
        part = pl.ds(first, hidden)
        for k, source in enumerate((wg_ref.at[part], wu_ref.at[part], wd_ref.at[:, part])):
            place, sem = held.at[k, part], sems.at[len(copies)]
            copies.append(
                (
                    pltpu.make_async_copy(source, place, sem),
                    pltpu.make_async_copy(place, out_ref.at[k, part], sem),
                )
            )
    for into, _ in copies:
        into.start()
    for into, out in copies:
        into.wait()
        out.start()
    for _, out in copies:
        out.wait()


def stack_weights(w_gate, w_up, w_down):
    width, hidden = w_gate.shape
    spec = pl.BlockSpec(memory_space=pl.ANY)
    return pl.pallas_call(
        stack_kernel,
        out_shape=jax.ShapeDtypeStruct((3, width, hidden), BF16),
        in_specs=[spec] * 3,
        out_specs=spec,
        scratch_shapes=[
            pltpu.VMEM((3, width, hidden), BF16),
            pltpu.SemaphoreType.DMA((3 * (width // hidden),)),
        ],
        compiler_params=params(56),
        cost_estimate=cost(0, 12 * width * hidden),
        name="stack_weights",
    )(w_gate, w_up, w_down)


def forward_kernel(rows, tokens_ref, *refs):
    out_ref = refs[-1]
    x, c = tokens_ref[0], tokens_ref[1]
    values = []
    wg_ref, wu_ref, wd_ref, pair_ref = refs[:4]
    hidden, width = wd_ref.shape
    values += [dot(x, w_ref[...], PLAIN) for w_ref in (wg_ref, wu_ref)]
    values.append(dot(c, wd_ref[...], INNER))
    values += [dot(x, pair_ref[i], PLAIN) for i in range(2)]
    blocks = [slice(first, first + hidden) for first in range(0, width, hidden)]
    products = [dot(c[:, b], pair_ref[2, b], INNER) for b in blocks]
    values.append(sum(products[1:], products[0]))
    cores, chunks = out_ref.shape[:2]
    for chunk in range(chunks):
        for core in range(cores):
            place = (chunk * cores + core) * rows
            put(out_ref, (core, chunk), [v[place : place + rows] for v in values], rows)


def forward(half, tokens, weights, held, rows, cores, chunks):
    hidden = weights[0].shape[1]
    coded = SUMS * rows + SCALES
    specs = [pl.BlockSpec(a.shape, lambda i, n=a.ndim: (0,) * n) for a in (tokens, *weights)]
    operands, alias = [tokens, *weights], {}
    if held is not None:
        operands.append(held)
        specs.append(pl.BlockSpec(memory_space=pl.ANY))
        alias = {5: 0}
    return pl.pallas_call(
        functools.partial(forward_kernel, rows),
        out_shape=jax.ShapeDtypeStruct((cores, chunks, coded, hidden), I16),
        grid=(1,),
        in_specs=specs,
        out_specs=pl.BlockSpec((cores, chunks // 2, coded, hidden), lambda i: (0, half, 0, 0)),
        input_output_aliases=alias,
        compiler_params=params(16),
        cost_estimate=cost(6 * tokens.size * hidden, 2 * tokens.size + 12 * weights[0].size),
        name="forward",
    )(*operands)


def core_sum_kernel(rows, in_ref, out_ref):
    for chunk in range(in_ref.shape[1]):
        both = [decode(in_ref[i, chunk], rows) for i in range(2)]
        put(out_ref, (chunk,), [a + b for a, b in zip(*both)], rows)


def core_sum(arrived, rows):
    return pl.pallas_call(
        functools.partial(core_sum_kernel, rows),
        out_shape=jax.ShapeDtypeStruct(arrived.shape[1:], I16),
        cost_estimate=cost(0, 3 * arrived.size),
        compiler_params=params(5),
        name="core_sum",
    )(arrived)


def pointwise_kernel(rows, in_ref, out_ref):
    parts = [decode(in_ref[i], rows) for i in range(in_ref.shape[0])]
    sums = [sum(p[1:], p[0]) for p in zip(*parts)]
    hidden = sums[0].shape[1]
    grads, kept = [], []
    for which in range(2):
        gate_pre, up_pre, grad_hidden = sums[3 * which : 3 * which + 3]
        sigmoid_gate = jax.nn.sigmoid(gate_pre)
        silu_gate = gate_pre * sigmoid_gate
        slope = sigmoid_gate * (1.0 + gate_pre * (1.0 - sigmoid_gate))
        grads += [grad_hidden * up_pre * slope, grad_hidden * silu_gate]
        kept.append(silu_gate * up_pre)
    lane = lax.broadcasted_iota(jnp.int32, (rows, 128), 1)
    exponents = jnp.zeros((rows, 128), F32)
    for k, v in enumerate(grads + kept):
        v = v.astype(BF16).astype(F32)
        exponent = exponent_of(v)
        exponents = jnp.where(lane == k, exponent, exponents)
        out_ref[:, k * hidden : (k + 1) * hidden] = integers(v, exponent)
    out_ref[:, SUMS * hidden :] = exponents.astype(jnp.int32).astype(I16)


def pointwise(arrived, rows):
    hidden = arrived.shape[2]
    return pl.pallas_call(
        functools.partial(pointwise_kernel, rows),
        out_shape=jax.ShapeDtypeStruct((rows, SUMS * hidden + 128), I16),
        compiler_params=params(4),
        cost_estimate=cost(0, 2 * arrived.size),
        name="pointwise",
    )(arrived)


def pieces(refs, which, columns):
    return jnp.concatenate([r[which, :, columns] for r in refs])


def gate_up_kernel(own_ref, pair_ref, *refs):
    *tokens, gate_ref, up_ref = refs
    hidden = gate_ref.shape[1]
    grads = jnp.concatenate([own_ref[:, : 2 * hidden], pair_ref[:, : 2 * hidden]])
    for first in range(0, gate_ref.shape[0], 256):
        columns = slice(first, first + 256)
        total = dot(pieces(tokens, 0, columns), grads, OUTER).astype(BF16)
        gate_ref[columns] = total[:, :hidden]
        up_ref[columns] = total[:, hidden:]


def gate_up_grads(own, pair, tokens):
    width, hidden = tokens[0].shape[2], own.shape[1] // SIDES
    return pl.pallas_call(
        gate_up_kernel,
        out_shape=(jax.ShapeDtypeStruct((width, hidden), BF16),) * 2,
        compiler_params=params(10),
        cost_estimate=cost(8 * own.shape[0] * hidden * width, 8 * tokens[0].size),
        name="gate_up_grads",
    )(own, pair, *tokens)


def down_kernel(own_ref, pair_ref, keep_ref, *refs):
    *tokens, out_ref = refs
    hidden = out_ref.shape[0]
    kept = [ref[:, 2 * hidden :] * keep_ref[i] for i, ref in enumerate((own_ref, pair_ref))]
    kept = jnp.concatenate(kept)
    for first in range(0, out_ref.shape[1], 256):
        columns = slice(first, first + 256)
        out_ref[:, columns] = dot(kept, pieces(tokens, 1, columns), OUTER).astype(BF16)


def down_grad(own, pair, keep, tokens):
    width, hidden = tokens[0].shape[2], own.shape[1] // SIDES
    return pl.pallas_call(
        down_kernel,
        out_shape=jax.ShapeDtypeStruct((hidden, width), BF16),
        compiler_params=params(9),
        cost_estimate=cost(4 * own.shape[0] * hidden * width, 8 * tokens[0].size),
        name="down_grad",
    )(own, pair, keep, *tokens)


def keep_of_tokens(keep_mask, x, tokens, nx, own_tokens, total):
    tiles, blocks = keep_mask.shape
    row = lax.broadcasted_iota(jnp.int32, (tokens, 1), 0)
    per_kind = tokens // 4
    place, eights = row % per_kind, per_kind // own_tokens * 8
    rest = place - eights
    z = 2 * jnp.where(rest < 0, place // 8, rest // 4) + row // per_kind % 2
    inside = jnp.where(rest < 0, place % 8, 8 + rest % 4)
    other = row // (2 * per_kind)
    from_x = x + other * (1 - 2 * (x % 2))
    tile = ((z * nx + from_x) * own_tokens + inside) // (total // tiles)
    chosen = tile == lax.broadcasted_iota(jnp.int32, (tokens, tiles), 1)
    keep = [
        jnp.sum(jnp.where(chosen, keep_mask[:, b][None, :], 0), axis=1, keepdims=True)
        for b in range(blocks)
    ]
    return jnp.concatenate([jnp.broadcast_to(k, (tokens, 128)) for k in keep], axis=1).astype(BF16)


def gathered_values(coded_ref, hidden, wanted):
    coded = coded_ref[...].reshape(coded_ref.shape[0] * coded_ref.shape[1], coded_ref.shape[2])
    scales = jnp.exp2(coded[:, SUMS * hidden :].astype(jnp.int32).astype(F32) - 15.0)
    values = []
    for k in wanted:
        v = coded[:, k * hidden : (k + 1) * hidden].astype(jnp.int32).astype(F32)
        values.append((v * scales[:, k : k + 1]).astype(BF16))
    return values


def sides_kernel(coded_ref, *side_refs):
    for which, side_ref in enumerate(side_refs):
        hidden = side_ref.shape[1] // SIDES
        values = gathered_values(coded_ref, hidden, (2 * which, 2 * which + 1, 4 + which))
        for i, v in enumerate(values):
            side_ref[:, i * hidden : (i + 1) * hidden] = v


def sides(coded, hidden):
    side = jax.ShapeDtypeStruct((coded.shape[0] * coded.shape[1], SIDES * hidden), BF16)
    return pl.pallas_call(
        sides_kernel,
        out_shape=(side, side),
        compiler_params=params(8),
        cost_estimate=cost(0, 4 * coded.size),
        name="sides",
    )(coded)


def input_grad_kernel(g_ref, wg_ref, wu_ref, pair_ref, out_ref):
    chunks, rows, width = out_ref.shape
    hidden = wg_ref.shape[1]
    xl = lax.axis_index("xl")
    g = gathered_values(g_ref, hidden, range(4))
    for first in range(0, width, 256):
        columns = slice(first, first + 256)
        places = (wg_ref[columns], wu_ref[columns], pair_ref[0, columns], pair_ref[1, columns])
        product = dot(g[0], places[0], INNER)
        for v, w in zip(g[1:], places[1:]):
            product = product + dot(v, w, INNER)
        product = product.astype(BF16)
        for k in range(2):
            owner = lax.rem(xl + k, 2)
            for odd in range(2):
                place = (2 * k + odd) * rows
                out_ref[2 * odd + owner, :, columns] = product[place : place + rows]


def input_grad(coded, weights, chunks):
    width, hidden = weights[0].shape
    tokens = coded.shape[0] * coded.shape[1]
    return pl.pallas_call(
        input_grad_kernel,
        out_shape=jax.ShapeDtypeStruct((chunks, tokens // chunks, width), BF16),
        compiler_params=params(12),
        cost_estimate=cost(8 * tokens * width * hidden, 2 * coded.size),
        name="input_grad",
    )(coded, *weights)


def x_sum_kernel(in_ref, out_ref):
    blocks = out_ref.shape[0]
    width = in_ref.shape[2]
    half = width // 2
    for first in range(0, blocks, 4):
        main = pl.ds(first * 8, 32)
        rest = pl.ds(blocks * 8 + first * 4, 16)
        main, rest = (
            sum((in_ref[i, rows].astype(F32) for i in range(1, in_ref.shape[0])), in_ref[0, rows].astype(F32))
            for rows in (main, rest)
        )
        for i in range(4):
            tail = rest[4 * i : 4 * i + 4]
            tail = jnp.concatenate([tail[:, :half], tail[:, half:]])
            block = jnp.concatenate([main[8 * i : 8 * i + 8], tail], axis=1)
            out_ref[first + i] = block.astype(BF16)


def x_sum(arrived, blocks):
    width = arrived.shape[2]
    return pl.pallas_call(
        x_sum_kernel,
        out_shape=jax.ShapeDtypeStruct((blocks, 8, 3 * width // 2), BF16),
        cost_estimate=cost(0, 2 * arrived.size),
        compiler_params=params(5),
        name="x_sum",
    )(arrived)


def z_sum_kernel(in_ref, out_ref):
    width = out_ref.shape[1]
    total = in_ref[0].astype(F32)
    for i in range(1, in_ref.shape[0]):
        total = total + in_ref[i].astype(F32)
    tail = jnp.concatenate([total[:4, width:], total[4:, width:]], axis=1)
    out_ref[...] = jnp.concatenate([total[:, :width], tail]).astype(BF16)


def z_sum(arrived, own_tokens, width):
    return pl.pallas_call(
        z_sum_kernel,
        out_shape=jax.ShapeDtypeStruct((own_tokens, width), BF16),
        cost_estimate=cost(0, 2 * arrived.size),
        compiler_params=params(3),
        name="z_sum",
    )(arrived)


def shards(inputs, cotangent, w_gate, w_up, w_down, keep_mask):
    own_tokens, width = inputs.shape
    hidden = w_gate.shape[1]
    nz, nx, ny, nc = 16, 4, 4, 2
    total = own_tokens * nz * nx
    tokens = total // 2
    rows = tokens // (ny * nc)

    def to_partner(a):
        return lax.ppermute(a, ("xh", "xl"), [(0, 3), (3, 0), (1, 2), (2, 1)])

    w_2 = to_partner(stack_weights(w_gate, w_up, w_down))
    along_z = lax.all_gather(pack(inputs, cotangent), ("zq", "zb"))
    own = pl.pallas_call(
        unpack_kernel,
        out_shape=jax.ShapeDtypeStruct((2, tokens // 2, width), BF16),
        cost_estimate=cost(0, 4 * tokens * width),
        compiler_params=params(6),
        name="unpack",
    )(along_z)
    other = lax.ppermute(own, "xl", ring(2, 1))
    weights = (w_gate, w_up, w_down, w_2)

    parts = forward(0, own, weights, None, rows, nc, ny)
    parts = forward(1, other, weights, parts, rows, nc, ny)
    summed = core_sum(lax.all_to_all(parts, "c", 0, 0), rows)
    own_2 = to_partner(own)
    summed, own_2 = lax.optimization_barrier((summed, own_2))
    coded = lax.all_gather(pointwise(lax.all_to_all(summed, "y", 0, 0), rows), ("y", "c"))
    result = input_grad(coded, (w_gate, w_up, w_2), nx)
    result, coded, own_2 = lax.optimization_barrier((result, coded, own_2))
    arrived = lax.all_to_all(result, ("zb", "xl"), 0, 0)
    other_2 = lax.ppermute(own_2, "xl", ring(2, 1))
    mine, pair = sides(coded, hidden)
    pair = to_partner(pair)
    x = lax.axis_index(("xh", "xl"))
    keep = jnp.stack(
        [
            keep_of_tokens(keep_mask, at, tokens, nx, own_tokens, total)
            for at in (x, nx - 1 - x)
        ]
    )
    arrived, keep = lax.optimization_barrier((arrived, keep))

    grad_sum = x_sum(arrived, nz // 2)
    grad_input = z_sum(lax.all_to_all(grad_sum, "zq", 0, 0), own_tokens, width)
    places = (own, other, own_2, other_2)
    grad_gate, grad_up = gate_up_grads(mine, pair, places)
    grad_down = down_grad(mine, pair, keep, places)
    return grad_input, grad_gate, grad_up, grad_down


def solution(mesh):
    fine = Mesh(mesh.devices.reshape(8, 2, 2, 2, 4, 2), ("zq", "zb", "xh", "xl", "y", "c"))
    hid, mdl = ("zq", "zb", "xh", "xl"), ("y", "c")
    placed = (P(hid, mdl), P(hid, mdl), P(mdl, hid), P(mdl, hid), P(hid, mdl), P(None, hid))
    return jax.shard_map(
        shards,
        mesh=fine,
        in_specs=placed,
        out_specs=(P(hid, mdl), P(mdl, hid), P(mdl, hid), P(hid, mdl)),
        check_vma=False,
    )
```

```python
import functools

import jax
import jax.numpy as jnp
from jax import lax
from jax.experimental import pallas as pl
from jax.experimental.pallas import tpu as pltpu
from jax.sharding import Mesh, PartitionSpec as P

F32, BF16, I16 = jnp.float32, jnp.bfloat16, jnp.int16
INNER = (((1,), (1,)), ((), ()))
PLAIN = (((1,), (0,)), ((), ()))
OUTER = (((0,), (0,)), ((), ()))
SUMS = 6
SIDES = 3
SCALES = 16


def ring(size, step):
    return [(i, (i + step) % size) for i in range(size)]


def dot(a, b, dims):
    return lax.dot_general(a, b, dims, preferred_element_type=F32)


def params(mebibytes):
    return pltpu.CompilerParams(vmem_limit_bytes=mebibytes << 20)


def cost(flops, moved):
    return pl.CostEstimate(flops=flops, bytes_accessed=moved, transcendentals=0)


def row_is_lane(rows, lanes):
    shape = (rows, lanes)
    return lax.broadcasted_iota(jnp.int32, shape, 0) == lax.broadcasted_iota(jnp.int32, shape, 1)


def exponent_of(values):
    most = jnp.max(jnp.abs(values), axis=1, keepdims=True)
    return jnp.ceil(jnp.log2(jnp.maximum(most, 1e-30)) + 0.01)


def integers(values, exponent):
    return jnp.round(values * jnp.exp2(15.0 - exponent)).astype(jnp.int32).astype(I16)


def code(values):
    rows, lanes = values[0].shape
    diagonal = row_is_lane(rows, lanes)
    place = lax.broadcasted_iota(jnp.int32, (SCALES, lanes), 0)
    codes, tile = [], jnp.zeros((SCALES, lanes), F32)
    for k, v in enumerate(values):
        exponent = exponent_of(v)
        codes.append(integers(v, exponent))
        along = jnp.sum(jnp.where(diagonal, exponent, 0.0), axis=0, keepdims=True)
        tile = jnp.where(place == k, along, tile)
    return codes, tile.astype(jnp.int32).astype(I16)


def decode(block, rows):
    lanes = block.shape[1]
    diagonal = row_is_lane(rows, lanes)
    tile = jnp.exp2(block[SUMS * rows :].astype(jnp.int32).astype(F32) - 15.0)
    out = []
    for k in range(SUMS):
        scale = jnp.sum(jnp.where(diagonal, tile[k : k + 1], 0.0), axis=1, keepdims=True)
        out.append(block[k * rows : (k + 1) * rows].astype(jnp.int32).astype(F32) * scale)
    return out


def put(out_ref, index, values, rows):
    codes, tile = code(values)
    for k, c in enumerate(codes):
        out_ref[(*index, pl.ds(k * rows, rows))] = c
    out_ref[(*index, pl.ds(SUMS * rows, SCALES))] = tile


def unpack_kernel(packed_ref, out_ref):
    blocks = packed_ref.shape[0] // 2
    width = out_ref.shape[2]
    for odd in range(2):
        base = odd * 12 * blocks
        for first in range(0, blocks, 2):
            pair = [packed_ref[2 * (first + i) + odd].astype(F32) for i in range(2)]
            for which in range(2):
                rows = jnp.concatenate([p[which * 8 : which * 8 + 8, :width] for p in pair])
                place = base + first * 8
                out_ref[which, place : place + 16] = rows.astype(BF16)
        for first in range(0, blocks, 4):
            four = [packed_ref[2 * (first + i) + odd, :, width:].astype(F32) for i in range(4)]
            for which in range(2):
                part = [p[which * 8 : which * 8 + 8] for p in four]
                halves = [jnp.concatenate([p[h : h + 4] for p in part]) for h in (0, 4)]
                place = base + 8 * blocks + first * 4
                out_ref[which, place : place + 16] = jnp.concatenate(halves, axis=1).astype(BF16)


def pack_kernel(*refs):
    packed = []
    for ref in refs[:-1]:
        a = ref[...].astype(F32)
        half = a.shape[1] // 2
        tail = jnp.concatenate([a[8:, :half], a[8:, half:]])
        packed.append(jnp.concatenate([a[:8], tail], axis=1))
    refs[-1][...] = jnp.concatenate(packed).astype(BF16)


def pack(*arrays):
    width = arrays[0].shape[1]
    return pl.pallas_call(
        pack_kernel,
        out_shape=jax.ShapeDtypeStruct((8 * len(arrays), 3 * width // 2), BF16),
        cost_estimate=cost(0, 48 * len(arrays) * width),
        compiler_params=params(2),
        name="pack",
    )(*arrays)


def stack_kernel(wg_ref, wu_ref, wd_ref, out_ref, held, sems):
    hidden, width = wd_ref.shape
    copies = []
    for first in range(0, width, hidden):
        part = pl.ds(first, hidden)
        for k, source in enumerate((wg_ref.at[part], wu_ref.at[part], wd_ref.at[:, part])):
            place, sem = held.at[k, part], sems.at[len(copies)]
            copies.append(
                (
                    pltpu.make_async_copy(source, place, sem),
                    pltpu.make_async_copy(place, out_ref.at[k, part], sem),
                )
            )
    for into, _ in copies:
        into.start()
    for into, out in copies:
        into.wait()
        out.start()
    for _, out in copies:
        out.wait()


def stack_weights(w_gate, w_up, w_down):
    width, hidden = w_gate.shape
    spec = pl.BlockSpec(memory_space=pl.ANY)
    return pl.pallas_call(
        stack_kernel,
        out_shape=jax.ShapeDtypeStruct((3, width, hidden), BF16),
        in_specs=[spec] * 3,
        out_specs=spec,
        scratch_shapes=[
            pltpu.VMEM((3, width, hidden), BF16),
            pltpu.SemaphoreType.DMA((3 * (width // hidden),)),
        ],
        compiler_params=params(56),
        cost_estimate=cost(0, 12 * width * hidden),
        name="stack_weights",
    )(w_gate, w_up, w_down)


def forward_kernel(rows, tokens_ref, *refs):
    out_ref = refs[-1]
    x, c = tokens_ref[0], tokens_ref[1]
    values = []
    wg_ref, wu_ref, wd_ref, pair_ref = refs[:4]
    hidden, width = wd_ref.shape
    values += [dot(x, w_ref[...], PLAIN) for w_ref in (wg_ref, wu_ref)]
    values.append(dot(c, wd_ref[...], INNER))
    values += [dot(x, pair_ref[i], PLAIN) for i in range(2)]
    blocks = [slice(first, first + hidden) for first in range(0, width, hidden)]
    products = [dot(c[:, b], pair_ref[2, b], INNER) for b in blocks]
    values.append(sum(products[1:], products[0]))
    cores, chunks = out_ref.shape[:2]
    for chunk in range(chunks):
        for core in range(cores):
            place = (chunk * cores + core) * rows
            put(out_ref, (core, chunk), [v[place : place + rows] for v in values], rows)


def forward(half, tokens, weights, held, rows, cores, chunks):
    hidden = weights[0].shape[1]
    coded = SUMS * rows + SCALES
    specs = [pl.BlockSpec(a.shape, lambda i, n=a.ndim: (0,) * n) for a in (tokens, *weights)]
    operands, alias = [tokens, *weights], {}
    if held is not None:
        operands.append(held)
        specs.append(pl.BlockSpec(memory_space=pl.ANY))
        alias = {5: 0}
    return pl.pallas_call(
        functools.partial(forward_kernel, rows),
        out_shape=jax.ShapeDtypeStruct((cores, chunks, coded, hidden), I16),
        grid=(1,),
        in_specs=specs,
        out_specs=pl.BlockSpec((cores, chunks // 2, coded, hidden), lambda i: (0, half, 0, 0)),
        input_output_aliases=alias,
        compiler_params=params(16),
        cost_estimate=cost(6 * tokens.size * hidden, 2 * tokens.size + 12 * weights[0].size),
        name="forward",
    )(*operands)


def core_sum_kernel(rows, in_ref, out_ref):
    for chunk in range(in_ref.shape[1]):
        both = [decode(in_ref[i, chunk], rows) for i in range(2)]
        put(out_ref, (chunk,), [a + b for a, b in zip(*both)], rows)


def core_sum(arrived, rows):
    return pl.pallas_call(
        functools.partial(core_sum_kernel, rows),
        out_shape=jax.ShapeDtypeStruct(arrived.shape[1:], I16),
        cost_estimate=cost(0, 3 * arrived.size),
        compiler_params=params(5),
        name="core_sum",
    )(arrived)


def pointwise_kernel(rows, in_ref, out_ref):
    parts = [decode(in_ref[i], rows) for i in range(in_ref.shape[0])]
    sums = [sum(p[1:], p[0]) for p in zip(*parts)]
    hidden = sums[0].shape[1]
    grads, kept = [], []
    for which in range(2):
        gate_pre, up_pre, grad_hidden = sums[3 * which : 3 * which + 3]
        sigmoid_gate = jax.nn.sigmoid(gate_pre)
        silu_gate = gate_pre * sigmoid_gate
        slope = sigmoid_gate * (1.0 + gate_pre * (1.0 - sigmoid_gate))
        grads += [grad_hidden * up_pre * slope, grad_hidden * silu_gate]
        kept.append(silu_gate * up_pre)
    lane = lax.broadcasted_iota(jnp.int32, (rows, 128), 1)
    exponents = jnp.zeros((rows, 128), F32)
    for k, v in enumerate(grads + kept):
        v = v.astype(BF16).astype(F32)
        exponent = exponent_of(v)
        exponents = jnp.where(lane == k, exponent, exponents)
        out_ref[:, k * hidden : (k + 1) * hidden] = integers(v, exponent)
    out_ref[:, SUMS * hidden :] = exponents.astype(jnp.int32).astype(I16)


def pointwise(arrived, rows):
    hidden = arrived.shape[2]
    return pl.pallas_call(
        functools.partial(pointwise_kernel, rows),
        out_shape=jax.ShapeDtypeStruct((rows, SUMS * hidden + 128), I16),
        compiler_params=params(4),
        cost_estimate=cost(0, 2 * arrived.size),
        name="pointwise",
    )(arrived)


def pieces(refs, which, columns):
    return jnp.concatenate([r[which, :, columns] for r in refs])


def gate_up_kernel(own_ref, pair_ref, *refs):
    *tokens, gate_ref, up_ref = refs
    hidden = gate_ref.shape[1]
    grads = jnp.concatenate([own_ref[:, : 2 * hidden], pair_ref[:, : 2 * hidden]])
    for first in range(0, gate_ref.shape[0], 256):
        columns = slice(first, first + 256)
        total = dot(pieces(tokens, 0, columns), grads, OUTER).astype(BF16)
        gate_ref[columns] = total[:, :hidden]
        up_ref[columns] = total[:, hidden:]


def gate_up_grads(own, pair, tokens):
    width, hidden = tokens[0].shape[2], own.shape[1] // SIDES
    return pl.pallas_call(
        gate_up_kernel,
        out_shape=(jax.ShapeDtypeStruct((width, hidden), BF16),) * 2,
        compiler_params=params(10),
        cost_estimate=cost(8 * own.shape[0] * hidden * width, 8 * tokens[0].size),
        name="gate_up_grads",
    )(own, pair, *tokens)


def down_kernel(own_ref, pair_ref, keep_ref, *refs):
    *tokens, out_ref = refs
    hidden = out_ref.shape[0]
    kept = [ref[:, 2 * hidden :] * keep_ref[i] for i, ref in enumerate((own_ref, pair_ref))]
    kept = jnp.concatenate(kept)
    for first in range(0, out_ref.shape[1], 256):
        columns = slice(first, first + 256)
        out_ref[:, columns] = dot(kept, pieces(tokens, 1, columns), OUTER).astype(BF16)


def down_grad(own, pair, keep, tokens):
    width, hidden = tokens[0].shape[2], own.shape[1] // SIDES
    return pl.pallas_call(
        down_kernel,
        out_shape=jax.ShapeDtypeStruct((hidden, width), BF16),
        compiler_params=params(9),
        cost_estimate=cost(4 * own.shape[0] * hidden * width, 8 * tokens[0].size),
        name="down_grad",
    )(own, pair, keep, *tokens)


def keep_of_tokens(keep_mask, x, tokens, nx, own_tokens, total):
    tiles, blocks = keep_mask.shape
    row = lax.broadcasted_iota(jnp.int32, (tokens, 1), 0)
    per_kind = tokens // 4
    place, eights = row % per_kind, per_kind // own_tokens * 8
    rest = place - eights
    z = 2 * jnp.where(rest < 0, place // 8, rest // 4) + row // per_kind % 2
    inside = jnp.where(rest < 0, place % 8, 8 + rest % 4)
    other = row // (2 * per_kind)
    from_x = x + other * (1 - 2 * (x % 2))
    tile = ((z * nx + from_x) * own_tokens + inside) // (total // tiles)
    chosen = tile == lax.broadcasted_iota(jnp.int32, (tokens, tiles), 1)
    keep = [
        jnp.sum(jnp.where(chosen, keep_mask[:, b][None, :], 0), axis=1, keepdims=True)
        for b in range(blocks)
    ]
    return jnp.concatenate([jnp.broadcast_to(k, (tokens, 128)) for k in keep], axis=1).astype(BF16)


def gathered_values(coded_ref, hidden, wanted):
    coded = coded_ref[...].reshape(coded_ref.shape[0] * coded_ref.shape[1], coded_ref.shape[2])
    scales = jnp.exp2(coded[:, SUMS * hidden :].astype(jnp.int32).astype(F32) - 15.0)
    values = []
    for k in wanted:
        v = coded[:, k * hidden : (k + 1) * hidden].astype(jnp.int32).astype(F32)
        values.append((v * scales[:, k : k + 1]).astype(BF16))
    return values


def sides_kernel(coded_ref, *side_refs):
    for which, side_ref in enumerate(side_refs):
        hidden = side_ref.shape[1] // SIDES
        values = gathered_values(coded_ref, hidden, (2 * which, 2 * which + 1, 4 + which))
        for i, v in enumerate(values):
            side_ref[:, i * hidden : (i + 1) * hidden] = v


def sides(coded, hidden):
    side = jax.ShapeDtypeStruct((coded.shape[0] * coded.shape[1], SIDES * hidden), BF16)
    return pl.pallas_call(
        sides_kernel,
        out_shape=(side, side),
        compiler_params=params(8),
        cost_estimate=cost(0, 4 * coded.size),
        name="sides",
    )(coded)


def input_grad_kernel(g_ref, wg_ref, wu_ref, pair_ref, out_ref):
    chunks, rows, width = out_ref.shape
    hidden = wg_ref.shape[1]
    xl = lax.axis_index("xl")
    g = gathered_values(g_ref, hidden, range(4))
    for first in range(0, width, 256):
        columns = slice(first, first + 256)
        places = (wg_ref[columns], wu_ref[columns], pair_ref[0, columns], pair_ref[1, columns])
        product = dot(g[0], places[0], INNER)
        for v, w in zip(g[1:], places[1:]):
            product = product + dot(v, w, INNER)
        product = product.astype(BF16)
        for k in range(2):
            owner = lax.rem(xl + k, 2)
            for odd in range(2):
                place = (2 * k + odd) * rows
                out_ref[2 * odd + owner, :, columns] = product[place : place + rows]


def input_grad(coded, weights, chunks):
    width, hidden = weights[0].shape
    tokens = coded.shape[0] * coded.shape[1]
    return pl.pallas_call(
        input_grad_kernel,
        out_shape=jax.ShapeDtypeStruct((chunks, tokens // chunks, width), BF16),
        compiler_params=params(12),
        cost_estimate=cost(8 * tokens * width * hidden, 2 * coded.size),
        name="input_grad",
    )(coded, *weights)


def x_sum_kernel(*refs):
    *in_refs, out_ref = refs
    blocks = out_ref.shape[0]
    half = in_refs[0].shape[1] // 2
    for first in range(0, blocks, 4):
        main = pl.ds(first * 8, 32)
        rest = pl.ds(blocks * 8 + first * 4, 16)
        main, rest = (
            sum((r[rows].astype(F32) for r in in_refs[1:]), in_refs[0][rows].astype(F32))
            for rows in (main, rest)
        )
        for i in range(4):
            tail = rest[4 * i : 4 * i + 4]
            tail = jnp.concatenate([tail[:, :half], tail[:, half:]])
            block = jnp.concatenate([main[8 * i : 8 * i + 8], tail], axis=1)
            out_ref[first + i] = block.astype(BF16)


def x_sum(arrived, blocks):
    parts, rows, width = arrived.shape
    return pl.pallas_call(
        x_sum_kernel,
        out_shape=jax.ShapeDtypeStruct((blocks, 8, 3 * width // 2), BF16),
        grid=(1,),
        in_specs=[pl.BlockSpec((None, rows, width), lambda i, k=k: (k, 0, 0)) for k in range(parts)],
        out_specs=pl.BlockSpec((blocks, 8, 3 * width // 2), lambda i: (0, 0, 0)),
        compiler_params=params(5),
        cost_estimate=cost(0, 2 * arrived.size),
        name="x_sum",
    )(*[arrived] * parts)


def z_sum_kernel(in_ref, out_ref):
    width = out_ref.shape[1]
    total = in_ref[0].astype(F32)
    for i in range(1, in_ref.shape[0]):
        total = total + in_ref[i].astype(F32)
    tail = jnp.concatenate([total[:4, width:], total[4:, width:]], axis=1)
    out_ref[...] = jnp.concatenate([total[:, :width], tail]).astype(BF16)


def z_sum(arrived, own_tokens, width):
    return pl.pallas_call(
        z_sum_kernel,
        out_shape=jax.ShapeDtypeStruct((own_tokens, width), BF16),
        cost_estimate=cost(0, 2 * arrived.size),
        compiler_params=params(3),
        name="z_sum",
    )(arrived)


def shards(inputs, cotangent, w_gate, w_up, w_down, keep_mask):
    own_tokens, width = inputs.shape
    hidden = w_gate.shape[1]
    nz, nx, ny, nc = 16, 4, 4, 2
    total = own_tokens * nz * nx
    tokens = total // 2
    rows = tokens // (ny * nc)

    def to_partner(a):
        return lax.ppermute(a, ("xh", "xl"), [(0, 3), (3, 0), (1, 2), (2, 1)])

    w_2 = to_partner(stack_weights(w_gate, w_up, w_down))
    along_z = lax.all_gather(pack(inputs, cotangent), ("zq", "zb"))
    own = pl.pallas_call(
        unpack_kernel,
        out_shape=jax.ShapeDtypeStruct((2, tokens // 2, width), BF16),
        cost_estimate=cost(0, 4 * tokens * width),
        compiler_params=params(6),
        name="unpack",
    )(along_z)
    other = lax.ppermute(own, "xl", ring(2, 1))
    weights = (w_gate, w_up, w_down, w_2)

    parts = forward(0, own, weights, None, rows, nc, ny)
    parts = forward(1, other, weights, parts, rows, nc, ny)
    summed = core_sum(lax.all_to_all(parts, "c", 0, 0), rows)
    own_2 = to_partner(own)
    summed, own_2 = lax.optimization_barrier((summed, own_2))
    coded = lax.all_gather(pointwise(lax.all_to_all(summed, "y", 0, 0), rows), ("y", "c"))
    result = input_grad(coded, (w_gate, w_up, w_2), nx)
    result, coded, own_2 = lax.optimization_barrier((result, coded, own_2))
    arrived = lax.all_to_all(result, ("zb", "xl"), 0, 0)
    other_2 = lax.ppermute(own_2, "xl", ring(2, 1))
    mine, pair = sides(coded, hidden)
    pair = to_partner(pair)
    x = lax.axis_index(("xh", "xl"))
    keep = jnp.stack(
        [
            keep_of_tokens(keep_mask, at, tokens, nx, own_tokens, total)
            for at in (x, nx - 1 - x)
        ]
    )
    arrived, keep = lax.optimization_barrier((arrived, keep))

    grad_sum = x_sum(arrived, nz // 2)
    grad_input = z_sum(lax.all_to_all(grad_sum, "zq", 0, 0), own_tokens, width)
    places = (own, other, own_2, other_2)
    grad_gate, grad_up = gate_up_grads(mine, pair, places)
    grad_down = down_grad(mine, pair, keep, places)
    return grad_input, grad_gate, grad_up, grad_down


def solution(mesh):
    fine = Mesh(mesh.devices.reshape(8, 2, 2, 2, 4, 2), ("zq", "zb", "xh", "xl", "y", "c"))
    hid, mdl = ("zq", "zb", "xh", "xl"), ("y", "c")
    placed = (P(hid, mdl), P(hid, mdl), P(mdl, hid), P(mdl, hid), P(hid, mdl), P(None, hid))
    return jax.shard_map(
        shards,
        mesh=fine,
        in_specs=placed,
        out_specs=(P(hid, mdl), P(mdl, hid), P(mdl, hid), P(hid, mdl)),
        check_vma=False,
    )
```

```python
import functools

import jax
import jax.numpy as jnp
from jax import lax
from jax.experimental import pallas as pl
from jax.experimental.pallas import tpu as pltpu
from jax.sharding import Mesh, PartitionSpec as P

F32, BF16, I16 = jnp.float32, jnp.bfloat16, jnp.int16
INNER = (((1,), (1,)), ((), ()))
PLAIN = (((1,), (0,)), ((), ()))
OUTER = (((0,), (0,)), ((), ()))
SUMS = 6
SIDES = 3
SCALES = 16


def ring(size, step):
    return [(i, (i + step) % size) for i in range(size)]


def dot(a, b, dims):
    return lax.dot_general(a, b, dims, preferred_element_type=F32)


def params(mebibytes):
    return pltpu.CompilerParams(vmem_limit_bytes=mebibytes << 20)


def cost(flops, moved):
    return pl.CostEstimate(flops=flops, bytes_accessed=moved, transcendentals=0)


def row_is_lane(rows, lanes):
    shape = (rows, lanes)
    return lax.broadcasted_iota(jnp.int32, shape, 0) == lax.broadcasted_iota(jnp.int32, shape, 1)


def exponent_of(values):
    most = jnp.max(jnp.abs(values), axis=1, keepdims=True)
    return jnp.ceil(jnp.log2(jnp.maximum(most, 1e-30)) + 0.01)


def integers(values, exponent):
    return jnp.round(values * jnp.exp2(15.0 - exponent)).astype(jnp.int32).astype(I16)


def code(values):
    rows, lanes = values[0].shape
    diagonal = row_is_lane(rows, lanes)
    place = lax.broadcasted_iota(jnp.int32, (SCALES, lanes), 0)
    codes, tile = [], jnp.zeros((SCALES, lanes), F32)
    for k, v in enumerate(values):
        exponent = exponent_of(v)
        codes.append(integers(v, exponent))
        along = jnp.sum(jnp.where(diagonal, exponent, 0.0), axis=0, keepdims=True)
        tile = jnp.where(place == k, along, tile)
    return codes, tile.astype(jnp.int32).astype(I16)


def decode(block, rows):
    lanes = block.shape[1]
    diagonal = row_is_lane(rows, lanes)
    tile = jnp.exp2(block[SUMS * rows :].astype(jnp.int32).astype(F32) - 15.0)
    out = []
    for k in range(SUMS):
        scale = jnp.sum(jnp.where(diagonal, tile[k : k + 1], 0.0), axis=1, keepdims=True)
        out.append(block[k * rows : (k + 1) * rows].astype(jnp.int32).astype(F32) * scale)
    return out


def put(out_ref, index, values, rows):
    codes, tile = code(values)
    for k, c in enumerate(codes):
        out_ref[(*index, pl.ds(k * rows, rows))] = c
    out_ref[(*index, pl.ds(SUMS * rows, SCALES))] = tile


def unpack_kernel(packed_ref, out_ref):
    blocks = packed_ref.shape[0] // 2
    width = out_ref.shape[2]
    for odd in range(2):
        base = odd * 12 * blocks
        for first in range(0, blocks, 2):
            pair = [packed_ref[2 * (first + i) + odd].astype(F32) for i in range(2)]
            for which in range(2):
                rows = jnp.concatenate([p[which * 8 : which * 8 + 8, :width] for p in pair])
                place = base + first * 8
                out_ref[which, place : place + 16] = rows.astype(BF16)
        for first in range(0, blocks, 4):
            four = [packed_ref[2 * (first + i) + odd, :, width:].astype(F32) for i in range(4)]
            for which in range(2):
                part = [p[which * 8 : which * 8 + 8] for p in four]
                halves = [jnp.concatenate([p[h : h + 4] for p in part]) for h in (0, 4)]
                place = base + 8 * blocks + first * 4
                out_ref[which, place : place + 16] = jnp.concatenate(halves, axis=1).astype(BF16)


def pack_kernel(*refs):
    packed = []
    for ref in refs[:-1]:
        a = ref[...].astype(F32)
        half = a.shape[1] // 2
        tail = jnp.concatenate([a[8:, :half], a[8:, half:]])
        packed.append(jnp.concatenate([a[:8], tail], axis=1))
    refs[-1][...] = jnp.concatenate(packed).astype(BF16)


def pack(*arrays):
    width = arrays[0].shape[1]
    return pl.pallas_call(
        pack_kernel,
        out_shape=jax.ShapeDtypeStruct((8 * len(arrays), 3 * width // 2), BF16),
        cost_estimate=cost(0, 48 * len(arrays) * width),
        compiler_params=params(2),
        name="pack",
    )(*arrays)


def stack_kernel(wg_ref, wu_ref, wd_ref, out_ref, held, sems):
    hidden, width = wd_ref.shape
    copies, half = [], hidden // 2
    for first in range(0, width, half):
        part = pl.ds(first, half)
        block, upper = pl.ds(first // hidden * hidden, hidden), pl.ds(first % hidden, half)
        for k, source in enumerate((wg_ref.at[part], wu_ref.at[part], wd_ref.at[upper, block])):
            place, sem = held.at[k, part], sems.at[len(copies)]
            copies.append(
                (
                    pltpu.make_async_copy(source, place, sem),
                    pltpu.make_async_copy(place, out_ref.at[k, part], sem),
                )
            )
    for into, _ in copies:
        into.start()
    for into, out in copies:
        into.wait()
        out.start()
    for _, out in copies:
        out.wait()


def stack_weights(w_gate, w_up, w_down):
    width, hidden = w_gate.shape
    spec = pl.BlockSpec(memory_space=pl.ANY)
    return pl.pallas_call(
        stack_kernel,
        out_shape=jax.ShapeDtypeStruct((3, width, hidden), BF16),
        in_specs=[spec] * 3,
        out_specs=spec,
        scratch_shapes=[
            pltpu.VMEM((3, width, hidden), BF16),
            pltpu.SemaphoreType.DMA((6 * (width // hidden),)),
        ],
        compiler_params=params(56),
        cost_estimate=cost(0, 12 * width * hidden),
        name="stack_weights",
    )(w_gate, w_up, w_down)


def forward_kernel(rows, tokens_ref, *refs):
    out_ref = refs[-1]
    x, c = tokens_ref[0], tokens_ref[1]
    values = []
    wg_ref, wu_ref, wd_ref, pair_ref = refs[:4]
    hidden, width = wd_ref.shape
    values += [dot(x, w_ref[...], PLAIN) for w_ref in (wg_ref, wu_ref)]
    values.append(dot(c, wd_ref[...], INNER))
    values += [dot(x, pair_ref[i], PLAIN) for i in range(2)]
    blocks = [slice(first, first + hidden) for first in range(0, width, hidden)]
    products = [dot(c[:, b], pair_ref[2, b], INNER) for b in blocks]
    values.append(sum(products[1:], products[0]))
    cores, chunks = out_ref.shape[:2]
    for chunk in range(chunks):
        for core in range(cores):
            place = (chunk * cores + core) * rows
            put(out_ref, (core, chunk), [v[place : place + rows] for v in values], rows)


def forward(half, tokens, weights, held, rows, cores, chunks):
    hidden = weights[0].shape[1]
    coded = SUMS * rows + SCALES
    specs = [pl.BlockSpec(a.shape, lambda i, n=a.ndim: (0,) * n) for a in (tokens, *weights)]
    operands, alias = [tokens, *weights], {}
    if held is not None:
        operands.append(held)
        specs.append(pl.BlockSpec(memory_space=pl.ANY))
        alias = {5: 0}
    return pl.pallas_call(
        functools.partial(forward_kernel, rows),
        out_shape=jax.ShapeDtypeStruct((cores, chunks, coded, hidden), I16),
        grid=(1,),
        in_specs=specs,
        out_specs=pl.BlockSpec((cores, chunks // 2, coded, hidden), lambda i: (0, half, 0, 0)),
        input_output_aliases=alias,
        compiler_params=params(16),
        cost_estimate=cost(6 * tokens.size * hidden, 2 * tokens.size + 12 * weights[0].size),
        name="forward",
    )(*operands)


def core_sum_kernel(rows, in_ref, out_ref):
    for chunk in range(in_ref.shape[1]):
        both = [decode(in_ref[i, chunk], rows) for i in range(2)]
        put(out_ref, (chunk,), [a + b for a, b in zip(*both)], rows)


def core_sum(arrived, rows):
    return pl.pallas_call(
        functools.partial(core_sum_kernel, rows),
        out_shape=jax.ShapeDtypeStruct(arrived.shape[1:], I16),
        cost_estimate=cost(0, 3 * arrived.size),
        compiler_params=params(5),
        name="core_sum",
    )(arrived)


def pointwise_kernel(rows, in_ref, out_ref):
    parts = [decode(in_ref[i], rows) for i in range(in_ref.shape[0])]
    sums = [sum(p[1:], p[0]) for p in zip(*parts)]
    hidden = sums[0].shape[1]
    grads, kept = [], []
    for which in range(2):
        gate_pre, up_pre, grad_hidden = sums[3 * which : 3 * which + 3]
        sigmoid_gate = jax.nn.sigmoid(gate_pre)
        silu_gate = gate_pre * sigmoid_gate
        slope = sigmoid_gate * (1.0 + gate_pre * (1.0 - sigmoid_gate))
        grads += [grad_hidden * up_pre * slope, grad_hidden * silu_gate]
        kept.append(silu_gate * up_pre)
    lane = lax.broadcasted_iota(jnp.int32, (rows, 128), 1)
    exponents = jnp.zeros((rows, 128), F32)
    for k, v in enumerate(grads + kept):
        v = v.astype(BF16).astype(F32)
        exponent = exponent_of(v)
        exponents = jnp.where(lane == k, exponent, exponents)
        out_ref[:, k * hidden : (k + 1) * hidden] = integers(v, exponent)
    out_ref[:, SUMS * hidden :] = exponents.astype(jnp.int32).astype(I16)


def pointwise(arrived, rows):
    hidden = arrived.shape[2]
    return pl.pallas_call(
        functools.partial(pointwise_kernel, rows),
        out_shape=jax.ShapeDtypeStruct((rows, SUMS * hidden + 128), I16),
        compiler_params=params(4),
        cost_estimate=cost(0, 2 * arrived.size),
        name="pointwise",
    )(arrived)


def pieces(refs, which, columns):
    return jnp.concatenate([r[which, :, columns] for r in refs])


def gate_up_kernel(own_ref, pair_ref, *refs):
    *tokens, gate_ref, up_ref = refs
    hidden = gate_ref.shape[1]
    grads = jnp.concatenate([own_ref[:, : 2 * hidden], pair_ref[:, : 2 * hidden]])
    for first in range(0, gate_ref.shape[0], 256):
        columns = slice(first, first + 256)
        total = dot(pieces(tokens, 0, columns), grads, OUTER).astype(BF16)
        gate_ref[columns] = total[:, :hidden]
        up_ref[columns] = total[:, hidden:]


def gate_up_grads(own, pair, tokens):
    width, hidden = tokens[0].shape[2], own.shape[1] // SIDES
    return pl.pallas_call(
        gate_up_kernel,
        out_shape=(jax.ShapeDtypeStruct((width, hidden), BF16),) * 2,
        compiler_params=params(10),
        cost_estimate=cost(8 * own.shape[0] * hidden * width, 8 * tokens[0].size),
        name="gate_up_grads",
    )(own, pair, *tokens)


def down_kernel(own_ref, pair_ref, keep_ref, *refs):
    *tokens, out_ref = refs
    hidden = out_ref.shape[0]
    kept = [ref[:, 2 * hidden :] * keep_ref[i] for i, ref in enumerate((own_ref, pair_ref))]
    kept = jnp.concatenate(kept)
    for first in range(0, out_ref.shape[1], 256):
        columns = slice(first, first + 256)
        out_ref[:, columns] = dot(kept, pieces(tokens, 1, columns), OUTER).astype(BF16)


def down_grad(own, pair, keep, tokens):
    width, hidden = tokens[0].shape[2], own.shape[1] // SIDES
    return pl.pallas_call(
        down_kernel,
        out_shape=jax.ShapeDtypeStruct((hidden, width), BF16),
        compiler_params=params(9),
        cost_estimate=cost(4 * own.shape[0] * hidden * width, 8 * tokens[0].size),
        name="down_grad",
    )(own, pair, keep, *tokens)


def keep_of_tokens(keep_mask, x, tokens, nx, own_tokens, total):
    tiles, blocks = keep_mask.shape
    row = lax.broadcasted_iota(jnp.int32, (tokens, 1), 0)
    per_kind = tokens // 4
    place, eights = row % per_kind, per_kind // own_tokens * 8
    rest = place - eights
    z = 2 * jnp.where(rest < 0, place // 8, rest // 4) + row // per_kind % 2
    inside = jnp.where(rest < 0, place % 8, 8 + rest % 4)
    other = row // (2 * per_kind)
    from_x = x + other * (1 - 2 * (x % 2))
    tile = ((z * nx + from_x) * own_tokens + inside) // (total // tiles)
    chosen = tile == lax.broadcasted_iota(jnp.int32, (tokens, tiles), 1)
    keep = [
        jnp.sum(jnp.where(chosen, keep_mask[:, b][None, :], 0), axis=1, keepdims=True)
        for b in range(blocks)
    ]
    return jnp.concatenate([jnp.broadcast_to(k, (tokens, 128)) for k in keep], axis=1).astype(BF16)


def gathered_values(coded_ref, hidden, wanted):
    coded = coded_ref[...].reshape(coded_ref.shape[0] * coded_ref.shape[1], coded_ref.shape[2])
    scales = jnp.exp2(coded[:, SUMS * hidden :].astype(jnp.int32).astype(F32) - 15.0)
    values = []
    for k in wanted:
        v = coded[:, k * hidden : (k + 1) * hidden].astype(jnp.int32).astype(F32)
        values.append((v * scales[:, k : k + 1]).astype(BF16))
    return values


def sides_kernel(coded_ref, *side_refs):
    for which, side_ref in enumerate(side_refs):
        hidden = side_ref.shape[1] // SIDES
        values = gathered_values(coded_ref, hidden, (2 * which, 2 * which + 1, 4 + which))
        for i, v in enumerate(values):
            side_ref[:, i * hidden : (i + 1) * hidden] = v


def sides(coded, hidden):
    side = jax.ShapeDtypeStruct((coded.shape[0] * coded.shape[1], SIDES * hidden), BF16)
    return pl.pallas_call(
        sides_kernel,
        out_shape=(side, side),
        compiler_params=params(8),
        cost_estimate=cost(0, 4 * coded.size),
        name="sides",
    )(coded)


def input_grad_kernel(g_ref, wg_ref, wu_ref, pair_ref, out_ref):
    chunks, rows, width = out_ref.shape
    hidden = wg_ref.shape[1]
    xl = lax.axis_index("xl")
    g = gathered_values(g_ref, hidden, range(4))
    for first in range(0, width, 256):
        columns = slice(first, first + 256)
        places = (wg_ref[columns], wu_ref[columns], pair_ref[0, columns], pair_ref[1, columns])
        product = dot(g[0], places[0], INNER)
        for v, w in zip(g[1:], places[1:]):
            product = product + dot(v, w, INNER)
        product = product.astype(BF16)
        for k in range(2):
            owner = lax.rem(xl + k, 2)
            for odd in range(2):
                place = (2 * k + odd) * rows
                out_ref[2 * odd + owner, :, columns] = product[place : place + rows]


def input_grad(coded, weights, chunks):
    width, hidden = weights[0].shape
    tokens = coded.shape[0] * coded.shape[1]
    return pl.pallas_call(
        input_grad_kernel,
        out_shape=jax.ShapeDtypeStruct((chunks, tokens // chunks, width), BF16),
        compiler_params=params(12),
        cost_estimate=cost(8 * tokens * width * hidden, 2 * coded.size),
        name="input_grad",
    )(coded, *weights)


def x_sum_kernel(*refs):
    *in_refs, out_ref = refs
    blocks = out_ref.shape[0]
    half = in_refs[0].shape[1] // 2
    for first in range(0, blocks, 4):
        main = pl.ds(first * 8, 32)
        rest = pl.ds(blocks * 8 + first * 4, 16)
        main, rest = (
            sum((r[rows].astype(F32) for r in in_refs[1:]), in_refs[0][rows].astype(F32))
            for rows in (main, rest)
        )
        for i in range(4):
            tail = rest[4 * i : 4 * i + 4]
            tail = jnp.concatenate([tail[:, :half], tail[:, half:]])
            block = jnp.concatenate([main[8 * i : 8 * i + 8], tail], axis=1)
            out_ref[first + i] = block.astype(BF16)


def x_sum(arrived, blocks):
    parts, rows, width = arrived.shape
    return pl.pallas_call(
        x_sum_kernel,
        out_shape=jax.ShapeDtypeStruct((blocks, 8, 3 * width // 2), BF16),
        grid=(1,),
        in_specs=[pl.BlockSpec((None, rows, width), lambda i, k=k: (k, 0, 0)) for k in range(parts)],
        out_specs=pl.BlockSpec((blocks, 8, 3 * width // 2), lambda i: (0, 0, 0)),
        compiler_params=params(5),
        cost_estimate=cost(0, 2 * arrived.size),
        name="x_sum",
    )(*[arrived] * parts)


def z_sum_kernel(in_ref, out_ref):
    width = out_ref.shape[1]
    total = in_ref[0].astype(F32)
    for i in range(1, in_ref.shape[0]):
        total = total + in_ref[i].astype(F32)
    tail = jnp.concatenate([total[:4, width:], total[4:, width:]], axis=1)
    out_ref[...] = jnp.concatenate([total[:, :width], tail]).astype(BF16)


def z_sum(arrived, own_tokens, width):
    return pl.pallas_call(
        z_sum_kernel,
        out_shape=jax.ShapeDtypeStruct((own_tokens, width), BF16),
        cost_estimate=cost(0, 2 * arrived.size),
        compiler_params=params(3),
        name="z_sum",
    )(arrived)


def shards(inputs, cotangent, w_gate, w_up, w_down, keep_mask):
    own_tokens, width = inputs.shape
    hidden = w_gate.shape[1]
    nz, nx, ny, nc = 16, 4, 4, 2
    total = own_tokens * nz * nx
    tokens = total // 2
    rows = tokens // (ny * nc)

    def to_partner(a):
        return lax.ppermute(a, ("xh", "xl"), [(0, 3), (3, 0), (1, 2), (2, 1)])

    w_2 = to_partner(stack_weights(w_gate, w_up, w_down))
    along_z = lax.all_gather(pack(inputs, cotangent), ("zq", "zb"))
    own = pl.pallas_call(
        unpack_kernel,
        out_shape=jax.ShapeDtypeStruct((2, tokens // 2, width), BF16),
        cost_estimate=cost(0, 4 * tokens * width),
        compiler_params=params(6),
        name="unpack",
    )(along_z)
    other = lax.ppermute(own, "xl", ring(2, 1))
    weights = (w_gate, w_up, w_down, w_2)

    parts = forward(0, own, weights, None, rows, nc, ny)
    parts = forward(1, other, weights, parts, rows, nc, ny)
    summed = core_sum(lax.all_to_all(parts, "c", 0, 0), rows)
    own_2 = to_partner(own)
    summed, own_2 = lax.optimization_barrier((summed, own_2))
    coded = lax.all_gather(pointwise(lax.all_to_all(summed, "y", 0, 0), rows), ("y", "c"))
    result = input_grad(coded, (w_gate, w_up, w_2), nx)
    result, coded, own_2 = lax.optimization_barrier((result, coded, own_2))
    arrived = lax.all_to_all(result, ("zb", "xl"), 0, 0)
    other_2 = lax.ppermute(own_2, "xl", ring(2, 1))
    mine, pair = sides(coded, hidden)
    pair = to_partner(pair)
    x = lax.axis_index(("xh", "xl"))
    keep = jnp.stack(
        [
            keep_of_tokens(keep_mask, at, tokens, nx, own_tokens, total)
            for at in (x, nx - 1 - x)
        ]
    )
    arrived, keep = lax.optimization_barrier((arrived, keep))

    grad_sum = x_sum(arrived, nz // 2)
    grad_input = z_sum(lax.all_to_all(grad_sum, "zq", 0, 0), own_tokens, width)
    places = (own, other, own_2, other_2)
    grad_gate, grad_up = gate_up_grads(mine, pair, places)
    grad_down = down_grad(mine, pair, keep, places)
    return grad_input, grad_gate, grad_up, grad_down


def solution(mesh):
    fine = Mesh(mesh.devices.reshape(8, 2, 2, 2, 4, 2), ("zq", "zb", "xh", "xl", "y", "c"))
    hid, mdl = ("zq", "zb", "xh", "xl"), ("y", "c")
    placed = (P(hid, mdl), P(hid, mdl), P(mdl, hid), P(mdl, hid), P(hid, mdl), P(None, hid))
    return jax.shard_map(
        shards,
        mesh=fine,
        in_specs=placed,
        out_specs=(P(hid, mdl), P(mdl, hid), P(mdl, hid), P(hid, mdl)),
        check_vma=False,
    )
```
